32 devices in a mesh: facet: 8 (over z, y), chan: 4 (over x, core).
Axes of the slice: x: 2, y: 2, z: 4, core: 2. Of those that a mesh axis runs over, the one named last changes fastest.
Arguments:
- taylor: float32 [8, 4, 4, 8192], P('facet', 'chan'), may hold values from -6 to 6
- chan_coord: float32 [4], replicated, may hold values from -1 to 1
- sub_offset: int32 [4, 2], replicated, may hold values from 0 to 65535
- sub_owner: int32 [4], replicated, may hold values from 0 to 7, as said below
- tile_list: int32 [128], P('facet'), may hold values from -1 to 127, as said below
- fourier: float32 [128, 4, 64, 256], P('facet', 'chan'), may hold values from -0.5 to 0.5
Outputs:
- visibilities: float32 [128, 4, 256], P('facet', 'chan')
The draws below stay inside these ranges and needn't reach their ends.
Inputs may be any that keep to these rules, and one draw needn't show every extreme that they name: `sub_owner`: every position along `facet` owns at most 2 of the listed subgrids, at least one owns exactly 2, and some own none. `tile_list`: on position i along `facet` every entry is -1 where i owns no subgrid, else lies in 0 .. 64 times the number of subgrids i owns, minus one.
All inputs are finite; a program needn't handle non-finite values.
Results may differ from the reference program's by a relative error of at most 0.0003.
Values sent between devices are 32-bit elements; how exact they have to be, the bound alone decides.
No kernel may reach another device: no remote copies, remote signals or barrier semaphores. Data moves between devices by JAX's collectives and lax.ppermute only.
A program may use at most 64 MiB of HBM per device.

```python
import math
import jax
import jax.numpy as jnp
from jax import lax

FACET = 8192
SIDE = 8
SKY = 65536
WIN = 64
VIS = 128
TAYLOR = 4
ROWS = 4
NBLK = 16
CAP = 2
BANDS = 8
CHANS = 4
SUBS = 4
N_FACET = 8
N_CHAN = 4


def owner_table(key):
    base_key = jax.random.fold_in(key, 7)
    key_full, key_bits, key_perm = jax.random.split(base_key, 3)
    slot_total = N_FACET * CAP
    full_owner = jax.random.randint(key_full, (), 0, N_FACET)
    slot_ids = jnp.arange(slot_total, dtype=jnp.int32)
    holders = slot_ids // CAP
    random_bits = jax.random.randint(key_bits, (slot_total,), 1, 2 ** 20)
    scores = jnp.where(holders == full_owner, 0, random_bits) * slot_total + slot_ids
    chosen = jnp.argsort(scores)[:SUBS]
    owners = (chosen // CAP).astype(jnp.int32)
    owners = jax.random.permutation(key_perm, owners)
    counts = jnp.sum((owners[None, :] == jnp.arange(N_FACET, dtype=jnp.int32)[:, None]).astype(jnp.int32), axis=1)
    return (owners, counts)


def draw_sub_owner(key, part):
    owners, counts = owner_table(key)
    return owners.astype(jnp.int32)


def draw_tile_list(key, part):
    owners, counts = owner_table(key)
    tile_key = jax.random.fold_in(key, 19)
    random_rows = jax.random.randint(tile_key, (N_FACET, NBLK), 0, 2 ** 20)
    limits = counts * WIN
    bounded = jnp.maximum(limits, 1)
    tiles = random_rows % bounded[:, None]
    tiles = tiles.at[:, 0].set(bounded - 1)
    tiles = tiles.at[:, 1].set(0)
    tiles = jnp.where(limits[:, None] > 0, tiles, -1)
    return tiles.reshape(N_FACET * NBLK).astype(jnp.int32)


def with_ends(drawn, own_key, least, top_value):
    longest = drawn.shape.index(max(drawn.shape))
    spots = []
    for shift in (0, 1):
        where = [jax.random.randint(jax.random.fold_in(own_key, axis), (), 0, length) for axis, length in enumerate(drawn.shape)]
        where[longest] = (where[longest] + shift) % drawn.shape[longest]
        spots.append(tuple(where))
    return drawn.at[spots[0]].set(least).at[spots[1]].set(top_value)


def shard_levels(key, extent, shards, low, largest):
    loudness, own = 1.0, jax.random.fold_in(key, 6)
    for dim, shards_of in shards:
        heights = jnp.exp(jax.random.uniform(jax.random.fold_in(own, dim), (shards_of,), jnp.float32, low / len(shards), largest / len(shards)))
        loudness = loudness * jnp.repeat(heights, extent[dim] // shards_of).reshape([-1 if axis == dim else 1 for axis in range(len(extent))])
    return loudness


def noise(stream_key, extent, width, limit, shards=(), held_as=jnp.bfloat16):
    factor_of = shard_levels(stream_key, extent, shards, -0.22, 0.18) if shards else 1.0
    drawn = jax.random.normal(stream_key, extent, jnp.float32) * width * factor_of
    return jnp.minimum(jnp.maximum(drawn, -limit), limit).astype(held_as)


def setup_inputs(seed: int = 0) -> dict:
    key_list = jax.random.split(jax.random.key(seed), 7)
    taylor = noise(key_list[0], (BANDS, TAYLOR, ROWS, FACET), 1.0, 6.0, ((0, 8), (1, 4)), jnp.float32)
    chan_coord = jnp.clip(jax.random.uniform(key_list[1], (CHANS,), jnp.float32, -1.0, 1.0), -1.0, 1.0)
    sub_offset = with_ends(jax.random.randint(key_list[2], (SUBS, 2), 0, SKY), jax.random.fold_in(key_list[2], 1), 0, SKY - 1).astype(jnp.int32)
    sub_owner = draw_sub_owner(jax.random.fold_in(key_list[6], 71), 0)
    tile_list = draw_tile_list(jax.random.fold_in(key_list[6], 71), 0)
    fourier = noise(key_list[5], (N_FACET * NBLK, CHANS, WIN, 2 * VIS), (2 * WIN) ** -0.5, 0.5, ((0, 8), (1, 4)), jnp.float32)
    return dict(taylor=taylor, chan_coord=chan_coord, sub_offset=sub_offset, sub_owner=sub_owner, tile_list=tile_list, fourier=fourier)


precise = lax.Precision.HIGHEST


def phase_index(left_side, right_side, period):
    low_part = left_side % 256
    high_part = left_side // 256
    wrapped = (low_part * right_side + ((high_part * right_side) % 256) * 256) % 65536
    return wrapped % period


def turn_angle(index_values, period):
    return (2.0 * math.pi / period) * index_values.astype(jnp.float32)


def taylor_powers(chan_coord, order_count):
    columns = [jnp.ones_like(chan_coord)]
    for degree in range(1, order_count):
        columns.append(columns[-1] * chan_coord)
    return jnp.stack(columns, axis=1)


def inverse_window(window, length):
    indices = jnp.arange(length, dtype=jnp.int32)
    angles = turn_angle((indices[:, None] * indices[None, :]) % length, length)
    cosines = jnp.cos(angles)
    sines = jnp.sin(angles)
    real_in = window[..., :length]
    imag_in = window[..., length:]
    real_mid = jnp.einsum("...vu,uw->...vw", real_in, cosines, precision=precise) - jnp.einsum("...vu,uw->...vw", imag_in, sines, precision=precise)
    imag_mid = jnp.einsum("...vu,uw->...vw", real_in, sines, precision=precise) + jnp.einsum("...vu,uw->...vw", imag_in, cosines, precision=precise)
    real_out = jnp.einsum("...vw,vy->...yw", real_mid, cosines, precision=precise) - jnp.einsum("...vw,vy->...yw", imag_mid, sines, precision=precise)
    imag_out = jnp.einsum("...vw,vy->...yw", real_mid, sines, precision=precise) + jnp.einsum("...vw,vy->...yw", imag_mid, cosines, precision=precise)
    return jnp.concatenate([real_out, imag_out], axis=-1) / length


def slot_ranks(sub_owner):
    positions = jnp.arange(sub_owner.shape[0], dtype=jnp.int32)
    earlier = positions[None, :] < positions[:, None]
    same_owner = sub_owner[None, :] == sub_owner[:, None]
    return jnp.sum((earlier & same_owner).astype(jnp.int32), axis=1)


def reference(taylor, chan_coord, sub_offset, sub_owner, tile_list, fourier):
    powers = taylor_powers(chan_coord, TAYLOR)
    channel = jnp.einsum("ct,ftrx->fcrx", powers, taylor, precision=precise)
    band_ids = jnp.arange(N_FACET, dtype=jnp.int32)
    facet_ids = band_ids % (SIDE * SIDE)
    anchor_x = (facet_ids % SIDE) * FACET
    anchor_y = (facet_ids // SIDE) * FACET + (band_ids // (SIDE * SIDE)) * ROWS
    flat_rows = channel.reshape(N_FACET * N_CHAN * ROWS, FACET)
    pixels = jnp.arange(FACET, dtype=jnp.int32)
    freq_steps = jnp.arange(WIN, dtype=jnp.int32)
    row_steps = jnp.arange(ROWS, dtype=jnp.int32)
    factor = float((FACET * ROWS * N_FACET) ** -0.5)

    def one_subgrid(offsets):
        column_freq = (offsets[0] + freq_steps) % SKY
        angles = turn_angle(phase_index(pixels[:, None], column_freq[None, :], SKY), SKY)
        lookup = jnp.concatenate([jnp.cos(angles), -jnp.sin(angles)], axis=1)
        partial_value = jnp.dot(flat_rows, lookup, precision=precise).reshape(N_FACET, N_CHAN, ROWS, 2 * WIN)
        shift_angle = turn_angle(phase_index(anchor_x[:, None], column_freq[None, :], SKY), SKY)[:, None, None, :]
        real_part = partial_value[..., :WIN]
        imag_part = partial_value[..., WIN:]
        real_x = real_part * jnp.cos(shift_angle) + imag_part * jnp.sin(shift_angle)
        imag_x = imag_part * jnp.cos(shift_angle) - real_part * jnp.sin(shift_angle)
        row_freq = (offsets[1] + freq_steps) % SKY
        row_pos = anchor_y[:, None] + row_steps[None, :]
        vertical = turn_angle(phase_index(row_pos[:, None, :], row_freq[None, :, None], SKY), SKY)
        cos_v = jnp.cos(vertical)
        sin_v = jnp.sin(vertical)
        real_w = jnp.einsum("nvr,ncru->cvu", cos_v, real_x, precision=precise) + jnp.einsum("nvr,ncru->cvu", sin_v, imag_x, precision=precise)
        imag_w = jnp.einsum("nvr,ncru->cvu", cos_v, imag_x, precision=precise) - jnp.einsum("nvr,ncru->cvu", sin_v, real_x, precision=precise)
        return jnp.concatenate([real_w, imag_w], axis=-1) * factor

    windows = lax.map(one_subgrid, sub_offset)
    pictures = inverse_window(windows, WIN)
    ranks = slot_ranks(sub_owner)
    tile_ids = tile_list.reshape(N_FACET, NBLK)
    usable = tile_ids >= 0
    clipped = jnp.maximum(tile_ids, 0)
    slot_index = clipped // WIN
    row_index = clipped % WIN
    sub_ids = jnp.arange(SUBS, dtype=jnp.int32)
    matches = (sub_owner[None, None, :] == band_ids[:, None, None]) & (ranks[None, None, :] == slot_index[:, :, None])
    chosen = jnp.sum(jnp.where(matches, sub_ids[None, None, :], 0), axis=2).astype(jnp.int32)
    picked = pictures[chosen, :, row_index, :]
    picked = jnp.where(usable[:, :, None, None], picked, 0.0)
    blocks = fourier.reshape(N_FACET, NBLK, N_CHAN, WIN, 2 * VIS)
    real_t = picked[..., :WIN]
    imag_t = picked[..., WIN:]
    real_f = blocks[..., :VIS]
    imag_f = blocks[..., VIS:]
    real_v = jnp.einsum("nbcy,nbcyz->nbcz", real_t, real_f, precision=precise) - jnp.einsum("nbcy,nbcyz->nbcz", imag_t, imag_f, precision=precise)
    imag_v = jnp.einsum("nbcy,nbcyz->nbcz", real_t, imag_f, precision=precise) + jnp.einsum("nbcy,nbcyz->nbcz", imag_t, real_f, precision=precise)
    return jnp.concatenate([real_v, imag_v], axis=-1).reshape(N_FACET * NBLK, N_CHAN, 2 * VIS)
```

```python
import jax
import jax.numpy as jnp
from jax import lax
from jax.sharding import PartitionSpec as P

FACET = 8192
SIDE = 8
SKY = 65536
WIN = 64
TAYLOR = 4

precise = lax.Precision.HIGHEST

SINE = (1.5707963705062866, -0.6459637880325317, 0.07968991994857788, -0.004674150608479977, 0.0001516751217423007)
COSINE = (0.9999999403953552, -1.2336982488632202, 0.2536506950855255, -0.020810570567846298, 0.0008581625297665596)


def turns(index):
    centred = ((index + SKY // 2) & (SKY - 1)) - SKY // 2
    z = centred.astype(jnp.float32) * (2.0 / SKY)
    w = z * z
    half_sin = z * (SINE[0] + w * (SINE[1] + w * (SINE[2] + w * (SINE[3] + w * SINE[4]))))
    half_cos = COSINE[0] + w * (COSINE[1] + w * (COSINE[2] + w * (COSINE[3] + w * COSINE[4])))
    return 1.0 - 2.0 * half_sin * half_sin, 2.0 * half_sin * half_cos


def column_transform(term, offsets, anchor_x):
    row_count, width = term.shape
    lane = 128
    folded = term.reshape(row_count, width // lane, lane).transpose(1, 0, 2).reshape(width // lane * row_count, lane)
    steps = jnp.arange(WIN, dtype=jnp.int32)
    freq = (offsets[:, 0:1] + steps[None, :]).reshape(-1)
    count = freq.shape[0]
    cos_fine, sin_fine = turns(jnp.arange(lane, dtype=jnp.int32)[:, None] * freq[None, :])
    lookup = jnp.concatenate([cos_fine, -sin_fine], axis=1)
    part = jnp.dot(folded, lookup, precision=precise).reshape(width // lane, row_count, 2 * count)
    start = anchor_x + lane * jnp.arange(width // lane, dtype=jnp.int32)
    cos_start, sin_start = turns(start[:, None] * freq[None, :])
    cos_start, sin_start = cos_start[:, None], sin_start[:, None]
    real, imag = part[..., :count], part[..., count:]
    return jnp.concatenate(
        [
            jnp.sum(real * cos_start + imag * sin_start, axis=0),
            jnp.sum(imag * cos_start - real * sin_start, axis=0),
        ],
        axis=1,
    )


def exchange(value, facets, chans, flip_facet, flip_chan):
    pairs = [
        (f * chans + c, (f ^ flip_facet) * chans + (c ^ flip_chan)) for f in range(facets) for c in range(chans)
    ]
    return lax.ppermute(value, ("facet", "chan"), pairs)


def gather_terms(part, facets, chans, band, chan):
    near = SIDE if facets > SIDE else facets
    odd = chan % 2 == 1
    other = exchange(part, facets, chans, 0, 1)
    both = jnp.concatenate([jnp.where(odd, other, part), jnp.where(odd, part, other)], axis=0)
    step = 1
    while step < near:
        both = both + exchange(both, facets, chans, step, 1)
        step *= 2
    blocks = both[None]
    place = chan // 2
    step = 2
    while step < chans:
        other = exchange(blocks, facets, chans, 0, step + 1)
        high = (chan // step) % 2 == 1
        blocks = jnp.concatenate([jnp.where(high, other, blocks), jnp.where(high, blocks, other)], axis=0)
        step *= 2
    terms = blocks.reshape(chans, part.shape[0], part.shape[1])
    if facets == near:
        return terms[None]
    groups = [[h * near + f for h in range(facets // near)] for f in range(near)]
    return lax.all_gather(terms, "facet", axis=0, axis_index_groups=groups)


def transform_blocks(blocks):
    vis = blocks.shape[2] // 2
    steps = jnp.arange(WIN, dtype=jnp.int32)
    cosines, sines = turns(steps[:, None] * steps[None, :] * (SKY // WIN))
    table = jnp.concatenate(
        [jnp.concatenate([cosines, -sines], axis=1), jnp.concatenate([sines, cosines], axis=1)], axis=0
    ) / WIN
    stacked = jnp.concatenate([blocks[..., :vis], blocks[..., vis:]], axis=1)
    out = jnp.einsum("uw,bwz->buz", table, stacked, precision=precise)
    return out[:, :WIN], out[:, WIN:]


def row_weights(tile_list, sub_offset, sub_owner, band, facets, row_count):
    subgrids = sub_owner.shape[0]
    order = jnp.arange(subgrids, dtype=jnp.int32)
    rank = jnp.sum((order[None, :] < order[:, None]) & (sub_owner[None, :] == sub_owner[:, None]), axis=1)
    tile = jnp.maximum(tile_list, 0)
    chosen = (sub_owner[None, :] == band) & (rank[None, :] == (tile // WIN)[:, None]) & (tile_list >= 0)[:, None]
    first_row = jnp.sum(jnp.where(chosen, sub_offset[None, :, 1], 0), axis=1)
    near = SIDE if facets > SIDE else facets
    group = jnp.arange(facets // near, dtype=jnp.int32)
    anchor = group % SIDE * FACET + group // SIDE * row_count
    position = (anchor[:, None] + jnp.arange(row_count, dtype=jnp.int32)[None, :]).reshape(-1)
    v = jnp.arange(WIN, dtype=jnp.int32)
    up = (tile % WIN)[:, None, None] * v[None, None, :] * (SKY // WIN)
    down = (first_row[:, None, None] + v[None, None, :]) * position[None, :, None]
    cosines, sines = turns(up - down)
    scale = float((FACET * row_count * facets) ** -0.5)
    return jnp.sum(cosines, axis=2) * scale, jnp.sum(sines, axis=2) * scale, chosen.astype(jnp.float32)


def local(taylor, chan_coord, sub_offset, sub_owner, tile_list, fourier):
    facets, chans = lax.axis_size("facet"), lax.axis_size("chan")
    band, chan = lax.axis_index("facet"), lax.axis_index("chan")
    row_count = taylor.shape[2]
    subgrids = sub_offset.shape[0]
    anchor_x = band % SIDE * FACET
    part = column_transform(taylor[0, 0], sub_offset, anchor_x)
    fourier_real, fourier_imag = transform_blocks(fourier[:, 0])
    real_a, imag_a, chosen = row_weights(tile_list, sub_offset, sub_owner, band, facets, row_count)
    coord = jnp.sum(jnp.where(jnp.arange(chan_coord.shape[0]) == chan, chan_coord, 0.0))
    powers = [jnp.ones((), jnp.float32)]
    for _ in range(1, TAYLOR):
        powers.append(powers[-1] * coord)
    terms = gather_terms(part, facets, chans, band, chan)
    mixed = sum(powers[t] * terms[:, t] for t in range(TAYLOR))
    mixed = mixed.reshape(-1, 2, subgrids, WIN)
    real_y = jnp.einsum("bs,qsu->bqu", chosen, mixed[:, 0], precision=precise)
    imag_y = jnp.einsum("bs,qsu->bqu", chosen, mixed[:, 1], precision=precise)
    real_t = jnp.sum(real_a[:, :, None] * real_y - imag_a[:, :, None] * imag_y, axis=1)
    imag_t = jnp.sum(real_a[:, :, None] * imag_y + imag_a[:, :, None] * real_y, axis=1)
    real_v = jnp.sum(real_t[:, :, None] * fourier_real - imag_t[:, :, None] * fourier_imag, axis=1)
    imag_v = jnp.sum(real_t[:, :, None] * fourier_imag + imag_t[:, :, None] * fourier_real, axis=1)
    return jnp.concatenate([real_v, imag_v], axis=-1)[:, None, :]


def solution(mesh):
    return jax.shard_map(
        local,
        mesh=mesh,
        in_specs=(
            P("facet", "chan", None, None),
            P(),
            P(),
            P(),
            P("facet"),
            P("facet", "chan", None, None),
        ),
        out_specs=P("facet", "chan", None),
        check_vma=False,
    )
```

```python
import functools
import math

import jax
import jax.numpy as jnp
from jax import lax
from jax.experimental import pallas as pl
from jax.experimental.pallas import tpu as pltpu
from jax.sharding import PartitionSpec as P

FACET = 8192
SIDE = 8
SKY = 65536
WIN = 64
TAYLOR = 4
LANE = 128

SINE = (1.5707963705062866, -0.6459637880325317, 0.07968991994857788, -0.004674150608479977, 0.0001516751217423007)
COSINE = (0.9999999403953552, -1.2336982488632202, 0.2536506950855255, -0.020810570567846298, 0.0008581625297665596)


def turns(index):
    centred = ((index + SKY // 2) & (SKY - 1)) - SKY // 2
    z = centred.astype(jnp.float32) * (2.0 / SKY)
    w = z * z
    half_sin = z * (SINE[0] + w * (SINE[1] + w * (SINE[2] + w * (SINE[3] + w * SINE[4]))))
    half_cos = COSINE[0] + w * (COSINE[1] + w * (COSINE[2] + w * (COSINE[3] + w * COSINE[4])))
    return 1.0 - 2.0 * half_sin * half_sin, 2.0 * half_sin * half_cos


def grant(*arrays):
    return (8 << 20) + 2 * sum(4 * math.prod(array.shape) for array in arrays)


def lasting(microseconds):
    return pl.CostEstimate(flops=int(microseconds * 1.15e9), bytes_accessed=0, transcendentals=0)


def split(value):
    high = value.astype(jnp.bfloat16)
    return high, (value - high.astype(jnp.float32)).astype(jnp.bfloat16)


def rotate(real, imag, cosines, sines):
    return real * cosines + imag * sines, imag * cosines - real * sines


def lookup_kernel(group, rows, offset_ref, look_ref, turn_ref):
    count = group * WIN
    step = turn_ref.shape[0] // 2 - 1
    anchor = lax.axis_index("facet") % SIDE * FACET
    lane_index = lax.broadcasted_iota(jnp.int32, (1, count), 1)
    pixel = lax.broadcasted_iota(jnp.int32, (LANE, count), 0)
    for first in range(0, offset_ref.shape[1], group):
        freq = lane_index % WIN
        for k in range(group):
            freq = freq + jnp.where(lane_index // WIN == k, offset_ref[0:1, first + k : first + k + 1], 0)
        cosines, sines = turns(pixel * freq)
        high, low = split(jnp.concatenate([cosines, -sines], axis=1))
        look_ref[0, :, 2 * first * WIN : 2 * first * WIN + 2 * count] = high
        look_ref[1, :, 2 * first * WIN : 2 * first * WIN + 2 * count] = low
        shifts = [LANE * step] + [anchor + k * LANE for k in range(step)]
        for k, shift in enumerate(shifts):
            cosines, sines = turns(freq * shift)
            turn_ref[2 * k : 2 * k + 1, first * WIN : first * WIN + count] = cosines
            turn_ref[2 * k + 1 : 2 * k + 2, first * WIN : first * WIN + count] = sines


def column_tables(offsets, rows):
    subgrids = offsets.shape[1]
    step = max(8 // rows, 1)
    shapes = [
        jax.ShapeDtypeStruct((2, LANE, 2 * subgrids * WIN), jnp.bfloat16),
        jax.ShapeDtypeStruct((2 + 2 * step, subgrids * WIN), jnp.float32),
    ]
    return pl.pallas_call(
        functools.partial(lookup_kernel, math.gcd(subgrids, 4), rows),
        in_specs=[pl.BlockSpec(memory_space=pltpu.VMEM)],
        out_specs=[pl.BlockSpec(memory_space=pltpu.VMEM)] * 2,
        out_shape=shapes,
        cost_estimate=lasting(0.3),
        compiler_params=pltpu.CompilerParams(vmem_limit_bytes=grant(*shapes)),
        name="column_tables",
    )(offsets)


def column_kernel(group, term_ref, look_ref, turn_ref, *refs):
    out_ref = refs[-1]
    rows, width = term_ref.shape[2:]
    count = group * WIN
    step = turn_ref.shape[0] // 2 - 1
    tall = step * rows
    folded = jnp.concatenate([term_ref[0, 0, :, k * LANE : (k + 1) * LANE] for k in range(width // LANE)], axis=0)
    term_high, term_low = split(folded)
    dot = functools.partial(jnp.dot, preferred_element_type=jnp.float32)
    for first in range(0, turn_ref.shape[1] // WIN, group):
        start = 2 * first * WIN
        look_high = look_ref[0, :, start : start + 2 * count]
        look_low = look_ref[1, :, start : start + 2 * count]
        part = dot(term_high, look_high) + (dot(term_low, look_high) + dot(term_high, look_low))
        turn = [turn_ref[k : k + 1, first * WIN : first * WIN + count] for k in range(turn_ref.shape[0])]
        real = jnp.zeros((tall, count), jnp.float32)
        imag = jnp.zeros((tall, count), jnp.float32)
        for k in reversed(range(width // LANE // step)):
            real, imag = rotate(real, imag, turn[0], turn[1])
            piece = part[k * tall : (k + 1) * tall]
            real, imag = real + piece[:, :count], imag + piece[:, count:]
        total_real = total_imag = 0.0
        for k in range(step):
            mine = slice(k * rows, (k + 1) * rows)
            piece = rotate(real[mine], imag[mine], turn[2 + 2 * k], turn[3 + 2 * k])
            total_real, total_imag = total_real + piece[0], total_imag + piece[1]
        out_ref[:, start : start + count] = total_real
        out_ref[:, start + count : start + 2 * count] = total_imag


def column_transform(taylor, tables, *early):
    rows, width = taylor.shape[2:]
    columns = tables[0].shape[2]
    return pl.pallas_call(
        functools.partial(column_kernel, math.gcd(columns // (2 * WIN), 4)),
        in_specs=[pl.BlockSpec(memory_space=pltpu.VMEM)] * (3 + len(early)),
        out_specs=pl.BlockSpec(memory_space=pltpu.VMEM),
        out_shape=jax.ShapeDtypeStruct((rows, columns), jnp.float32),
        cost_estimate=lasting(0.45),
        compiler_params=pltpu.CompilerParams(vmem_limit_bytes=grant(taylor, *tables, *early)),
        name="column_transform",
    )(taylor, *tables, *early)


def exchange(value, facets, chans, flip_facet, flip_chan):
    pairs = [
        (f * chans + c, (f ^ flip_facet) * chans + (c ^ flip_chan)) for f in range(facets) for c in range(chans)
    ]
    return lax.ppermute(value, ("facet", "chan"), pairs)


def gather_terms(both, facets, chans):
    near = SIDE if facets > SIDE else facets
    step = 1
    while step < near:
        both = both + exchange(both, facets, chans, step, 1)
        step *= 2
    pieces = [both]
    step = 2
    while step < chans:
        pieces = pieces + [exchange(piece, facets, chans, 0, step + 1) for piece in pieces]
        step *= 2
    if facets == near:
        return [piece[None] for piece in pieces]
    groups = [[h * near + f for h in range(facets // near)] for f in range(near)]
    return [lax.all_gather(piece, "facet", axis=0, axis_index_groups=groups) for piece in pieces]


def weight_kernel(rows, offset_hbm, owner_hbm, tile_hbm, coord_hbm, row_ref, mask_ref, mix_ref, *scratch):
    hbm = (offset_hbm, owner_hbm, tile_hbm, coord_hbm)
    offset_ref, owner_ref, tile_ref, coord_ref, sems = scratch
    copies = [pltpu.make_async_copy(a, b, sems.at[k]) for k, (a, b) in enumerate(zip(hbm, scratch[:4]))]
    for copy in copies:
        copy.start()
    facets = lax.axis_size("facet")
    band, chan = lax.axis_index("facet"), lax.axis_index("chan")

    for copy in copies:
        copy.wait()

    blocks = tile_ref.shape[0]
    sublane = lax.broadcasted_iota(jnp.int32, (blocks, LANE), 0)
    lane = lax.broadcasted_iota(jnp.int32, (blocks, LANE), 1)
    tile = jnp.zeros((blocks, LANE), jnp.int32)
    for b in range(blocks):
        tile = jnp.where(sublane == b, tile_ref[b], tile)
    slot = jnp.where(tile < 0, -1, tile // WIN)
    first_row = jnp.zeros((blocks, LANE), jnp.int32)
    seen = jnp.int32(0)
    for pair in range(0, owner_ref.shape[0], LANE // WIN):
        mask = jnp.zeros((blocks, LANE), jnp.float32)
        for k in range(LANE // WIN):
            owned = owner_ref[pair + k] == band
            chosen = slot == jnp.where(owned, seen, -2)
            seen = seen + jnp.where(owned, 1, 0)
            first_row = jnp.where(chosen, offset_ref[1, pair + k], first_row)
            mask = jnp.where(chosen & (lane // WIN == k), 1.0, mask)
        mask_ref[:, pair * WIN : pair * WIN + LANE] = mask

    scale = float((FACET * rows * facets) ** -0.5)
    v = lane % WIN
    up = jnp.maximum(tile, 0) % WIN * v * (SKY // WIN)
    near = SIDE if facets > SIDE else facets
    for h in range(facets // near):
        for r in range(rows):
            position = h % SIDE * FACET + h // SIDE * rows + r
            cosines, sines = turns(up - (first_row + v) * position)
            for part, value in enumerate((cosines, sines)):
                total = jnp.sum(jnp.where(lane < WIN, value, 0.0), axis=1, keepdims=True) * scale
                row_ref[part, h * rows + r] = jnp.broadcast_to(total, (blocks, LANE))

    coord = coord_ref[chan]
    tall = lax.broadcasted_iota(jnp.int32, (2 * rows, LANE), 0)
    for k in range(mix_ref.shape[0]):
        term = 2 * ((chan // 2) ^ k) + tall // rows
        power = jnp.ones((2 * rows, LANE), jnp.float32)
        for degree in range(1, TAYLOR):
            power = jnp.where(term >= degree, power * coord, power)
        mix_ref[k] = power


def finish_weights(offsets, owner, tiles, coord, facets, chans, rows):
    subgrids = owner.shape[0]
    blocks = tiles.shape[0]
    near = SIDE if facets > SIDE else facets
    shapes = [
        jax.ShapeDtypeStruct((2, facets // near * rows, blocks, LANE), jnp.float32),
        jax.ShapeDtypeStruct((blocks, subgrids * WIN), jnp.float32),
        jax.ShapeDtypeStruct((chans // 2, 2 * rows, LANE), jnp.float32),
    ]
    return pl.pallas_call(
        functools.partial(weight_kernel, rows),
        in_specs=[pl.BlockSpec(memory_space=pl.ANY)] * 4,
        out_specs=[pl.BlockSpec(memory_space=pltpu.VMEM)] * 3,
        out_shape=shapes,
        scratch_shapes=[
            pltpu.SMEM(offsets.shape, jnp.int32),
            pltpu.SMEM(owner.shape, jnp.int32),
            pltpu.SMEM(tiles.shape, jnp.int32),
            pltpu.SMEM(coord.shape, jnp.float32),
            pltpu.SemaphoreType.DMA((4,)),
        ],
        cost_estimate=lasting(0.75),
        compiler_params=pltpu.CompilerParams(vmem_limit_bytes=grant(*shapes)),
        name="finish_weights",
    )(offsets, owner, tiles, coord)


def finish_kernel(pieces, *refs):
    piece_refs = refs[:pieces]
    row_ref, mask_ref, mix_ref, block_ref, out_ref = refs[pieces:]
    groups, tall, width = piece_refs[0].shape
    rows = tall // 2
    subgrids = mask_ref.shape[1] // WIN
    group = math.gcd(subgrids, 4)
    count = group * WIN
    blocks = mask_ref.shape[0]
    real_row = imag_row = 0.0
    for first in range(0, subgrids, group):
        start = 2 * first * WIN
        real_t = imag_t = 0.0
        for h in range(groups):
            mixed = 0.0
            for k in range(pieces):
                weight = jnp.tile(mix_ref[k], (1, 2 * count // LANE))
                mixed = mixed + piece_refs[k][h, :, start : start + 2 * count] * weight
            mixed = mixed[:rows] + mixed[rows:]
            for r in range(rows):
                real_a = jnp.tile(row_ref[0, h * rows + r], (1, count // LANE))
                imag_a = jnp.tile(row_ref[1, h * rows + r], (1, count // LANE))
                real_y, imag_y = mixed[r : r + 1, :count], mixed[r : r + 1, count:]
                real_t = real_t + (real_a * real_y - imag_a * imag_y)
                imag_t = imag_t + (real_a * imag_y + imag_a * real_y)
        mask = mask_ref[:, first * WIN : first * WIN + count]
        for k in range(0, count, LANE):
            real_row = real_row + (real_t * mask)[:, k : k + LANE]
            imag_row = imag_row + (imag_t * mask)[:, k : k + LANE]
    row = jnp.concatenate(
        [sum(value[:, k : k + WIN] for k in range(0, LANE, WIN)) for value in (real_row, imag_row)], axis=1
    ).T
    vis = block_ref.shape[2]
    for b in range(blocks):
        real_c, imag_c = row[:WIN, b : b + 1], row[WIN:, b : b + 1]
        real_f, imag_f = block_ref[b, :WIN], block_ref[b, WIN:]
        out_ref[b, :, :vis] = jnp.sum(real_c * real_f - imag_c * imag_f, axis=0, keepdims=True)
        out_ref[b, :, vis:] = jnp.sum(real_c * imag_f + imag_c * real_f, axis=0, keepdims=True)


def finish(pieces, weights, transformed):
    blocks, _, vis = transformed.shape
    return pl.pallas_call(
        functools.partial(finish_kernel, len(pieces)),
        in_specs=[pl.BlockSpec(memory_space=pltpu.VMEM)] * (len(pieces) + 4),
        out_specs=pl.BlockSpec(memory_space=pltpu.VMEM),
        out_shape=jax.ShapeDtypeStruct((blocks, 1, 2 * vis), jnp.float32),
        cost_estimate=lasting(1.3),
        compiler_params=pltpu.CompilerParams(vmem_limit_bytes=grant(*pieces, *weights, transformed)),
        name="finish",
    )(*pieces, *weights, transformed)


def block_kernel(fourier_ref, out_ref):
    vis = out_ref.shape[2]
    here = lax.broadcasted_iota(jnp.int32, (2 * WIN, 2 * WIN), 0)
    there = lax.broadcasted_iota(jnp.int32, (2 * WIN, 2 * WIN), 1)
    cosines, sines = turns((here % WIN) * (there % WIN) * (SKY // WIN))
    sines = jnp.where(here < WIN, -sines, sines)
    table_high, table_low = split(jnp.where((here < WIN) == (there < WIN), cosines, sines) * (1.0 / WIN))
    dot = functools.partial(jnp.dot, preferred_element_type=jnp.float32)
    for b in range(0, out_ref.shape[0], 2):
        pair = [
            jnp.concatenate([fourier_ref[k, 0, :, :vis], fourier_ref[k, 0, :, vis:]], axis=0) for k in (b, b + 1)
        ]
        high, low = split(jnp.concatenate(pair, axis=1))
        done = dot(table_high, high) + (dot(table_low, high) + dot(table_high, low))
        out_ref[b] = done[:, :vis]
        out_ref[b + 1] = done[:, vis:]


def transform_blocks(fourier):
    blocks, _, _, width = fourier.shape
    vis = width // 2
    return pl.pallas_call(
        block_kernel,
        in_specs=[pl.BlockSpec(memory_space=pltpu.VMEM)],
        out_specs=pl.BlockSpec(memory_space=pltpu.VMEM),
        out_shape=jax.ShapeDtypeStruct((blocks, 2 * WIN, vis), jnp.float32),
        cost_estimate=lasting(0.65),
        compiler_params=pltpu.CompilerParams(vmem_limit_bytes=grant(fourier)),
        name="transform_blocks",
    )(fourier)


def local(taylor, chan_coord, sub_offset, sub_owner, tile_list, fourier):
    facets, chans = lax.axis_size("facet"), lax.axis_size("chan")
    chan = lax.axis_index("chan")
    offsets = sub_offset.T
    tables = column_tables(offsets, taylor.shape[2])
    beside = exchange(taylor, facets, chans, 0, 1)
    own, other = column_transform(taylor, tables), column_transform(beside, tables, fourier)
    odd = chan % 2 == 1
    both = jnp.concatenate([jnp.where(odd, other, own), jnp.where(odd, own, other)], axis=0)
    transformed = transform_blocks(fourier)
    weights = finish_weights(offsets, sub_owner, tile_list, chan_coord, facets, chans, taylor.shape[2])
    pieces = gather_terms(both, facets, chans)
    return finish(pieces, weights, transformed)


def solution(mesh):
    return jax.shard_map(
        local,
        mesh=mesh,
        in_specs=(
            P("facet", "chan", None, None),
            P(),
            P(),
            P(),
            P("facet"),
            P("facet", "chan", None, None),
        ),
        out_specs=P("facet", "chan", None),
        check_vma=False,
    )
```

```python
import functools
import math

import jax
import jax.numpy as jnp
from jax import lax
from jax.experimental import pallas as pl
from jax.experimental.pallas import tpu as pltpu
from jax.sharding import PartitionSpec as P

FACET = 8192
SIDE = 8
SKY = 65536
WIN = 64
TAYLOR = 4
LANE = 128
BLOCK = 256

SINE = (1.5707963705062866, -0.6459637880325317, 0.07968991994857788, -0.004674150608479977, 0.0001516751217423007)
COSINE = (0.9999999403953552, -1.2336982488632202, 0.2536506950855255, -0.020810570567846298, 0.0008581625297665596)


def turns(index):
    centred = ((index + SKY // 2) & (SKY - 1)) - SKY // 2
    z = centred.astype(jnp.float32) * (2.0 / SKY)
    w = z * z
    half_sin = z * (SINE[0] + w * (SINE[1] + w * (SINE[2] + w * (SINE[3] + w * SINE[4]))))
    half_cos = COSINE[0] + w * (COSINE[1] + w * (COSINE[2] + w * (COSINE[3] + w * COSINE[4])))
    return 1.0 - 2.0 * half_sin * half_sin, 2.0 * half_sin * half_cos


def grant(*arrays):
    return (8 << 20) + 2 * sum(4 * math.prod(array.shape) for array in arrays)


def lasting(microseconds):
    return pl.CostEstimate(flops=int(microseconds * 1.15e9), bytes_accessed=0, transcendentals=0)


def split(value):
    high = value.astype(jnp.bfloat16)
    return high, (value - high.astype(jnp.float32)).astype(jnp.bfloat16)


def rotate(real, imag, cosines, sines):
    return real * cosines + imag * sines, imag * cosines - real * sines


def write_tables(group, anchor, offset_ref, look_ref, turn_ref):
    count = group * WIN
    step = turn_ref.shape[0] // 2 - 1
    lane_index = lax.broadcasted_iota(jnp.int32, (1, count), 1)
    pixel = lax.broadcasted_iota(jnp.int32, (LANE, count), 0)
    for first in range(0, offset_ref.shape[1], group):
        freq = lane_index % WIN
        for k in range(group):
            freq = freq + jnp.where(lane_index // WIN == k, offset_ref[0, first + k], 0)
        cosines, sines = turns(pixel * freq)
        tables = [(cosines, -sines)]
        for k in range(LANE, BLOCK, LANE):
            tables.append(rotate(*tables[0], *turns(freq * k)))
        table = jnp.concatenate([jnp.concatenate(pair, axis=1) for pair in tables], axis=0)
        high, low = split(table)
        look_ref[0, :, 2 * first * WIN : 2 * first * WIN + 2 * count] = high
        look_ref[1, :, 2 * first * WIN : 2 * first * WIN + 2 * count] = low
        shifts = [BLOCK * step] + [anchor + k * BLOCK for k in range(step)]
        for k, shift in enumerate(shifts):
            cosines, sines = turns(freq * shift)
            turn_ref[2 * k : 2 * k + 1, first * WIN : first * WIN + count] = cosines
            turn_ref[2 * k + 1 : 2 * k + 2, first * WIN : first * WIN + count] = sines


def write_columns(group, term_ref, look_ref, turn_ref, out_ref):
    rows, width = term_ref.shape[2:]
    count = group * WIN
    step = turn_ref.shape[0] // 2 - 1
    tall = step * rows
    folded = jnp.concatenate([term_ref[0, 0, :, k * BLOCK : (k + 1) * BLOCK] for k in range(width // BLOCK)], axis=0)
    term_high, term_low = split(folded)
    dot = functools.partial(jnp.dot, preferred_element_type=jnp.float32)
    for first in range(0, turn_ref.shape[1] // WIN, group):
        start = 2 * first * WIN
        look_high = look_ref[0, :, start : start + 2 * count]
        look_low = look_ref[1, :, start : start + 2 * count]
        part = dot(term_high, look_high) + (dot(term_low, look_high) + dot(term_high, look_low))
        turn = [turn_ref[k : k + 1, first * WIN : first * WIN + count] for k in range(turn_ref.shape[0])]
        real = jnp.zeros((tall, count), jnp.float32)
        imag = jnp.zeros((tall, count), jnp.float32)
        for k in reversed(range(width // BLOCK // step)):
            real, imag = rotate(real, imag, turn[0], turn[1])
            piece = part[k * tall : (k + 1) * tall]
            real, imag = real + piece[:, :count], imag + piece[:, count:]
        total_real = total_imag = 0.0
        for k in range(step):
            mine = slice(k * rows, (k + 1) * rows)
            piece = rotate(real[mine], imag[mine], turn[2 + 2 * k], turn[3 + 2 * k])
            total_real, total_imag = total_real + piece[0], total_imag + piece[1]
        out_ref[:, start : start + count] = total_real
        out_ref[:, start + count : start + 2 * count] = total_imag


def own_kernel(group, offset_hbm, term_hbm, fourier_hbm, look_ref, turn_ref, out_ref, block_ref, *scratch):
    offset_ref, term_ref, sems = scratch
    moves = ((offset_hbm, offset_ref), (term_hbm, term_ref), (fourier_hbm, block_ref))
    copies = [pltpu.make_async_copy(a, b, sems.at[k]) for k, (a, b) in enumerate(moves)]
    for copy in copies:
        copy.start()
    anchor = lax.axis_index("facet") % SIDE * FACET
    copies[0].wait()
    write_tables(group, anchor, offset_ref, look_ref, turn_ref)
    copies[1].wait()
    write_columns(group, term_ref, look_ref, turn_ref, out_ref)
    copies[2].wait()


def own_columns(offsets, taylor, fourier):
    rows = taylor.shape[2]
    subgrids = offsets.shape[1]
    step = max(8 // rows, 1)
    shapes = [
        jax.ShapeDtypeStruct((2, BLOCK, 2 * subgrids * WIN), jnp.bfloat16),
        jax.ShapeDtypeStruct((2 + 2 * step, subgrids * WIN), jnp.float32),
        jax.ShapeDtypeStruct((rows, 2 * subgrids * WIN), jnp.float32),
        jax.ShapeDtypeStruct(fourier.shape, jnp.float32),
    ]
    return pl.pallas_call(
        functools.partial(own_kernel, math.gcd(subgrids, 4)),
        in_specs=[pl.BlockSpec(memory_space=pltpu.HBM)] * 3,
        out_specs=[pl.BlockSpec(memory_space=pltpu.VMEM)] * 4,
        out_shape=shapes,
        scratch_shapes=[
            pltpu.SMEM(offsets.shape, jnp.int32),
            pltpu.VMEM(taylor.shape, jnp.float32),
            pltpu.SemaphoreType.DMA((3,)),
        ],
        cost_estimate=lasting(1.4),
        compiler_params=pltpu.CompilerParams(vmem_limit_bytes=grant(*shapes)),
        name="own_columns",
    )(*(pltpu.with_memory_space_constraint(array, pltpu.HBM) for array in (offsets, taylor, fourier)))


def column_transform(taylor, tables):
    rows, width = taylor.shape[2:]
    columns = tables[0].shape[2]
    return pl.pallas_call(
        functools.partial(write_columns, math.gcd(columns // (2 * WIN), 4)),
        in_specs=[pl.BlockSpec(memory_space=pltpu.VMEM)] * 3,
        out_specs=pl.BlockSpec(memory_space=pltpu.VMEM),
        out_shape=jax.ShapeDtypeStruct((rows, columns), jnp.float32),
        cost_estimate=lasting(0.35),
        compiler_params=pltpu.CompilerParams(vmem_limit_bytes=grant(taylor, *tables)),
        name="column_transform",
    )(taylor, *tables)


def exchange(value, facets, chans, flip_facet, flip_chan):
    pairs = [
        (f * chans + c, (f ^ flip_facet) * chans + (c ^ flip_chan)) for f in range(facets) for c in range(chans)
    ]
    return lax.ppermute(value, ("facet", "chan"), pairs)


def gather_terms(both, facets, chans):
    near = SIDE if facets > SIDE else facets
    step = 1
    while step < near:
        both = both + exchange(both, facets, chans, step, 1)
        step *= 2
    pieces = [both]
    step = 2
    while step < chans:
        pieces = pieces + [exchange(piece, facets, chans, 0, step + 1) for piece in pieces]
        step *= 2
    if facets == near:
        return [piece[None] for piece in pieces]
    groups = [[h * near + f for h in range(facets // near)] for f in range(near)]
    return [lax.all_gather(piece, "facet", axis=0, axis_index_groups=groups) for piece in pieces]


def weight_kernel(rows, offset_hbm, owner_hbm, tile_hbm, coord_hbm, row_ref, mask_ref, mix_ref, *scratch):
    hbm = (offset_hbm, owner_hbm, tile_hbm, coord_hbm)
    offset_ref, owner_ref, tile_ref, coord_ref, sems = scratch
    copies = [pltpu.make_async_copy(a, b, sems.at[k]) for k, (a, b) in enumerate(zip(hbm, scratch[:4]))]
    for copy in copies:
        copy.start()
    facets = lax.axis_size("facet")
    band, chan = lax.axis_index("facet"), lax.axis_index("chan")

    for copy in copies:
        copy.wait()

    blocks = tile_ref.shape[0]
    sublane = lax.broadcasted_iota(jnp.int32, (blocks, LANE), 0)
    lane = lax.broadcasted_iota(jnp.int32, (blocks, LANE), 1)
    tile = jnp.zeros((blocks, LANE), jnp.int32)
    for b in range(blocks):
        tile = jnp.where(sublane == b, tile_ref[b], tile)
    slot = jnp.where(tile < 0, -1, tile // WIN)
    first_row = jnp.zeros((blocks, LANE), jnp.int32)
    seen = jnp.int32(0)
    for pair in range(0, owner_ref.shape[0], LANE // WIN):
        mask = jnp.zeros((blocks, LANE), jnp.float32)
        for k in range(LANE // WIN):
            owned = owner_ref[pair + k] == band
            chosen = slot == jnp.where(owned, seen, -2)
            seen = seen + jnp.where(owned, 1, 0)
            first_row = jnp.where(chosen, offset_ref[1, pair + k], first_row)
            mask = jnp.where(chosen & (lane // WIN == k), 1.0, mask)
        mask_ref[:, pair * WIN : pair * WIN + LANE] = mask

    scale = float((FACET * rows * facets) ** -0.5)
    v = lane % WIN
    up = jnp.maximum(tile, 0) % WIN * v * (SKY // WIN)
    near = SIDE if facets > SIDE else facets
    for h in range(facets // near):
        for r in range(rows):
            position = h % SIDE * FACET + h // SIDE * rows + r
            cosines, sines = turns(up - (first_row + v) * position)
            for part, value in enumerate((cosines, sines)):
                total = jnp.sum(jnp.where(lane < WIN, value, 0.0), axis=1, keepdims=True) * scale
                row_ref[part, h * rows + r] = jnp.broadcast_to(total, (blocks, LANE))

    coord = coord_ref[chan]
    tall = lax.broadcasted_iota(jnp.int32, (2 * rows, LANE), 0)
    for k in range(mix_ref.shape[0]):
        term = 2 * ((chan // 2) ^ k) + tall // rows
        power = jnp.ones((2 * rows, LANE), jnp.float32)
        for degree in range(1, TAYLOR):
            power = jnp.where(term >= degree, power * coord, power)
        mix_ref[k] = power


def finish_weights(offsets, owner, tiles, coord, facets, chans, rows):
    subgrids = owner.shape[0]
    blocks = tiles.shape[0]
    near = SIDE if facets > SIDE else facets
    shapes = [
        jax.ShapeDtypeStruct((2, facets // near * rows, blocks, LANE), jnp.float32),
        jax.ShapeDtypeStruct((blocks, subgrids * WIN), jnp.float32),
        jax.ShapeDtypeStruct((chans // 2, 2 * rows, LANE), jnp.float32),
    ]
    return pl.pallas_call(
        functools.partial(weight_kernel, rows),
        in_specs=[pl.BlockSpec(memory_space=pl.ANY)] * 4,
        out_specs=[pl.BlockSpec(memory_space=pltpu.VMEM)] * 3,
        out_shape=shapes,
        scratch_shapes=[
            pltpu.SMEM(offsets.shape, jnp.int32),
            pltpu.SMEM(owner.shape, jnp.int32),
            pltpu.SMEM(tiles.shape, jnp.int32),
            pltpu.SMEM(coord.shape, jnp.float32),
            pltpu.SemaphoreType.DMA((4,)),
        ],
        cost_estimate=lasting(0.75),
        compiler_params=pltpu.CompilerParams(vmem_limit_bytes=grant(*shapes)),
        name="finish_weights",
    )(offsets, owner, tiles, coord)


def finish_kernel(pieces, *refs):
    piece_refs = refs[:pieces]
    row_ref, mask_ref, mix_ref, block_ref, out_ref = refs[pieces:]
    groups, tall, width = piece_refs[0].shape
    rows = tall // 2
    subgrids = mask_ref.shape[1] // WIN
    group = math.gcd(subgrids, 4)
    count = group * WIN
    blocks = mask_ref.shape[0]
    real_row = imag_row = 0.0
    for first in range(0, subgrids, group):
        start = 2 * first * WIN
        real_t = imag_t = 0.0
        for h in range(groups):
            mixed = 0.0
            for k in range(pieces):
                weight = jnp.tile(mix_ref[k], (1, 2 * count // LANE))
                mixed = mixed + piece_refs[k][h, :, start : start + 2 * count] * weight
            mixed = mixed[:rows] + mixed[rows:]
            for r in range(rows):
                real_a = jnp.tile(row_ref[0, h * rows + r], (1, count // LANE))
                imag_a = jnp.tile(row_ref[1, h * rows + r], (1, count // LANE))
                real_y, imag_y = mixed[r : r + 1, :count], mixed[r : r + 1, count:]
                real_t = real_t + (real_a * real_y - imag_a * imag_y)
                imag_t = imag_t + (real_a * imag_y + imag_a * real_y)
        mask = mask_ref[:, first * WIN : first * WIN + count]
        for k in range(0, count, LANE):
            real_row = real_row + (real_t * mask)[:, k : k + LANE]
            imag_row = imag_row + (imag_t * mask)[:, k : k + LANE]
    row = jnp.concatenate(
        [sum(value[:, k : k + WIN] for k in range(0, LANE, WIN)) for value in (real_row, imag_row)], axis=1
    ).T
    vis = block_ref.shape[2]
    for b in range(blocks):
        real_c, imag_c = row[:WIN, b : b + 1], row[WIN:, b : b + 1]
        real_f, imag_f = block_ref[b, :WIN], block_ref[b, WIN:]
        out_ref[b, :, :vis] = jnp.sum(real_c * real_f - imag_c * imag_f, axis=0, keepdims=True)
        out_ref[b, :, vis:] = jnp.sum(real_c * imag_f + imag_c * real_f, axis=0, keepdims=True)


def finish(pieces, weights, transformed):
    blocks, _, vis = transformed.shape
    return pl.pallas_call(
        functools.partial(finish_kernel, len(pieces)),
        in_specs=[pl.BlockSpec(memory_space=pltpu.VMEM)] * (len(pieces) + 4),
        out_specs=pl.BlockSpec(memory_space=pltpu.VMEM),
        out_shape=jax.ShapeDtypeStruct((blocks, 1, 2 * vis), jnp.float32),
        cost_estimate=lasting(1.3),
        compiler_params=pltpu.CompilerParams(vmem_limit_bytes=grant(*pieces, *weights, transformed)),
        name="finish",
    )(*pieces, *weights, transformed)


def block_kernel(fourier_ref, out_ref):
    vis = out_ref.shape[2]
    here = lax.broadcasted_iota(jnp.int32, (2 * WIN, 2 * WIN), 0)
    there = lax.broadcasted_iota(jnp.int32, (2 * WIN, 2 * WIN), 1)
    cosines, sines = turns((here % WIN) * (there % WIN) * (SKY // WIN))
    sines = jnp.where(here < WIN, -sines, sines)
    table_high, table_low = split(jnp.where((here < WIN) == (there < WIN), cosines, sines) * (1.0 / WIN))
    dot = functools.partial(jnp.dot, preferred_element_type=jnp.float32)
    for b in range(0, out_ref.shape[0], 2):
        pair = [
            jnp.concatenate([fourier_ref[k, 0, :, :vis], fourier_ref[k, 0, :, vis:]], axis=0) for k in (b, b + 1)
        ]
        high, low = split(jnp.concatenate(pair, axis=1))
        done = dot(table_high, high) + (dot(table_low, high) + dot(table_high, low))
        out_ref[b] = done[:, :vis]
        out_ref[b + 1] = done[:, vis:]


def transform_blocks(fourier):
    blocks, _, _, width = fourier.shape
    vis = width // 2
    return pl.pallas_call(
        block_kernel,
        in_specs=[pl.BlockSpec(memory_space=pltpu.VMEM)],
        out_specs=pl.BlockSpec(memory_space=pltpu.VMEM),
        out_shape=jax.ShapeDtypeStruct((blocks, 2 * WIN, vis), jnp.float32),
        cost_estimate=lasting(0.65),
        compiler_params=pltpu.CompilerParams(vmem_limit_bytes=grant(fourier)),
        name="transform_blocks",
    )(fourier)


def local(taylor, chan_coord, sub_offset, sub_owner, tile_list, fourier):
    facets, chans = lax.axis_size("facet"), lax.axis_size("chan")
    chan = lax.axis_index("chan")
    offsets = sub_offset.T
    beside = exchange(taylor, facets, chans, 0, 1)
    *tables, own, blocks = own_columns(offsets, taylor, fourier)
    other = column_transform(beside, tables)
    odd = chan % 2 == 1
    both = jnp.concatenate([jnp.where(odd, other, own), jnp.where(odd, own, other)], axis=0)
    transformed = transform_blocks(blocks)
    weights = finish_weights(offsets, sub_owner, tile_list, chan_coord, facets, chans, taylor.shape[2])
    pieces = gather_terms(both, facets, chans)
    return finish(pieces, weights, transformed)


def solution(mesh):
    return jax.shard_map(
        local,
        mesh=mesh,
        in_specs=(
            P("facet", "chan", None, None),
            P(),
            P(),
            P(),
            P("facet"),
            P("facet", "chan", None, None),
        ),
        out_specs=P("facet", "chan", None),
        check_vma=False,
    )
```

```python
import functools
import math

import jax
import jax.numpy as jnp
from jax import lax
from jax.experimental import pallas as pl
from jax.experimental.pallas import tpu as pltpu
from jax.sharding import PartitionSpec as P

FACET = 8192
SIDE = 8
SKY = 65536
WIN = 64
TAYLOR = 4
LANE = 128
BLOCK = 256

SINE = (1.5707963705062866, -0.6459637880325317, 0.07968991994857788, -0.004674150608479977, 0.0001516751217423007)
COSINE = (0.9999999403953552, -1.2336982488632202, 0.2536506950855255, -0.020810570567846298, 0.0008581625297665596)


def turns(index):
    centred = ((index + SKY // 2) & (SKY - 1)) - SKY // 2
    z = centred.astype(jnp.float32) * (2.0 / SKY)
    w = z * z
    half_sin = z * (SINE[0] + w * (SINE[1] + w * (SINE[2] + w * (SINE[3] + w * SINE[4]))))
    half_cos = COSINE[0] + w * (COSINE[1] + w * (COSINE[2] + w * (COSINE[3] + w * COSINE[4])))
    return 1.0 - 2.0 * half_sin * half_sin, 2.0 * half_sin * half_cos


def grant(*arrays):
    return (8 << 20) + 2 * sum(4 * math.prod(array.shape) for array in arrays)


def lasting(microseconds):
    return pl.CostEstimate(flops=int(microseconds * 1.15e9), bytes_accessed=0, transcendentals=0)


def split(value):
    high = value.astype(jnp.bfloat16)
    return high, (value - high.astype(jnp.float32)).astype(jnp.bfloat16)


def rotate(real, imag, cosines, sines):
    return real * cosines + imag * sines, imag * cosines - real * sines


def write_tables(group, anchor, offset_ref, look_ref, turn_ref):
    count = group * WIN
    step = turn_ref.shape[0] // 2 - 1
    lane_index = lax.broadcasted_iota(jnp.int32, (1, count), 1)
    sublane = lax.broadcasted_iota(jnp.int32, (8, count), 0)
    shifts = [8, 16, 32, BLOCK * step] + [anchor + k * BLOCK for k in range(step)]
    shift = sum(jnp.where(sublane == k, value, 0) for k, value in enumerate(shifts))
    for first in range(0, offset_ref.shape[1], group):
        freq = lane_index % WIN
        for k in range(group):
            freq = freq + jnp.where(lane_index // WIN == k, offset_ref[0, first + k], 0)
        cosines, sines = turns(shift * freq)
        hops = [(cosines[k : k + 1], sines[k : k + 1]) for k in range(len(shifts))]
        cosines, sines = turns(sublane * freq)
        tables = [(cosines, -sines)]
        for k in range(2):
            tables = tables + [rotate(*table, *hops[k]) for table in tables]
        while len(tables) < BLOCK // 8:
            tables.append(rotate(*tables[-4], *hops[2]))
        for part in (0, 1):
            high, low = split(jnp.concatenate([table[part] for table in tables], axis=0))
            start = (2 * first + part * group) * WIN
            look_ref[0, :, start : start + count] = high
            look_ref[1, :, start : start + count] = low
        for k, hop in enumerate(hops[3:]):
            for part in (0, 1):
                turn_ref[2 * k + part : 2 * k + part + 1, first * WIN : first * WIN + count] = hop[part]


def write_columns(group, term_ref, look_ref, turn_ref, out_ref):
    rows, width = term_ref.shape[2:]
    count = group * WIN
    step = turn_ref.shape[0] // 2 - 1
    tall = step * rows
    folded = jnp.concatenate([term_ref[0, 0, :, k * BLOCK : (k + 1) * BLOCK] for k in range(width // BLOCK)], axis=0)
    term_high, term_low = split(folded)
    dot = functools.partial(jnp.dot, preferred_element_type=jnp.float32)
    for first in range(0, turn_ref.shape[1] // WIN, group):
        start = 2 * first * WIN
        look_high = look_ref[0, :, start : start + 2 * count]
        look_low = look_ref[1, :, start : start + 2 * count]
        part = dot(term_high, look_high) + (dot(term_low, look_high) + dot(term_high, look_low))
        turn = [turn_ref[k : k + 1, first * WIN : first * WIN + count] for k in range(turn_ref.shape[0])]
        real = jnp.zeros((tall, count), jnp.float32)
        imag = jnp.zeros((tall, count), jnp.float32)
        for k in reversed(range(width // BLOCK // step)):
            real, imag = rotate(real, imag, turn[0], turn[1])
            piece = part[k * tall : (k + 1) * tall]
            real, imag = real + piece[:, :count], imag + piece[:, count:]
        total_real = total_imag = 0.0
        for k in range(step):
            mine = slice(k * rows, (k + 1) * rows)
            piece = rotate(real[mine], imag[mine], turn[2 + 2 * k], turn[3 + 2 * k])
            total_real, total_imag = total_real + piece[0], total_imag + piece[1]
        out_ref[:, start : start + count] = total_real
        out_ref[:, start + count : start + 2 * count] = total_imag


def own_kernel(group, offset_hbm, term_hbm, look_ref, turn_ref, out_ref, *scratch):
    offset_ref, term_ref, sems = scratch
    moves = ((offset_hbm, offset_ref), (term_hbm, term_ref))
    copies = [pltpu.make_async_copy(a, b, sems.at[k]) for k, (a, b) in enumerate(moves)]
    for copy in copies:
        copy.start()
    anchor = lax.axis_index("facet") % SIDE * FACET
    copies[0].wait()
    write_tables(group, anchor, offset_ref, look_ref, turn_ref)
    copies[1].wait()
    write_columns(group, term_ref, look_ref, turn_ref, out_ref)


def own_columns(offsets, taylor):
    rows = taylor.shape[2]
    subgrids = offsets.shape[1]
    step = max(8 // rows, 1)
    shapes = [
        jax.ShapeDtypeStruct((2, BLOCK, 2 * subgrids * WIN), jnp.bfloat16),
        jax.ShapeDtypeStruct((2 + 2 * step, subgrids * WIN), jnp.float32),
        jax.ShapeDtypeStruct((rows, 2 * subgrids * WIN), jnp.float32),
    ]
    return pl.pallas_call(
        functools.partial(own_kernel, math.gcd(subgrids, 4)),
        in_specs=[pl.BlockSpec(memory_space=pltpu.HBM)] * 2,
        out_specs=[pl.BlockSpec(memory_space=pltpu.VMEM)] * 3,
        out_shape=shapes,
        scratch_shapes=[
            pltpu.SMEM(offsets.shape, jnp.int32),
            pltpu.VMEM(taylor.shape, jnp.float32),
            pltpu.SemaphoreType.DMA((2,)),
        ],
        cost_estimate=lasting(1.4),
        compiler_params=pltpu.CompilerParams(vmem_limit_bytes=grant(*shapes)),
        name="own_columns",
    )(*(pltpu.with_memory_space_constraint(array, pltpu.HBM) for array in (offsets, taylor)))


def column_transform(taylor, tables):
    rows, width = taylor.shape[2:]
    columns = tables[0].shape[2]
    return pl.pallas_call(
        functools.partial(write_columns, math.gcd(columns // (2 * WIN), 4)),
        in_specs=[pl.BlockSpec(memory_space=pltpu.VMEM)] * 3,
        out_specs=pl.BlockSpec(memory_space=pltpu.VMEM),
        out_shape=jax.ShapeDtypeStruct((rows, columns), jnp.float32),
        cost_estimate=lasting(0.35),
        compiler_params=pltpu.CompilerParams(vmem_limit_bytes=grant(taylor, *tables)),
        name="column_transform",
    )(taylor, *tables)


def exchange(value, facets, chans, flip_facet, flip_chan):
    pairs = [
        (f * chans + c, (f ^ flip_facet) * chans + (c ^ flip_chan)) for f in range(facets) for c in range(chans)
    ]
    return lax.ppermute(value, ("facet", "chan"), pairs)


def gather_terms(both, facets, chans):
    near = SIDE if facets > SIDE else facets
    step = 1
    while step < near:
        both = both + exchange(both, facets, chans, step, 1)
        step *= 2
    pieces = [both]
    step = 2
    while step < chans:
        pieces = pieces + [exchange(piece, facets, chans, 0, step + 1) for piece in pieces]
        step *= 2
    if facets == near:
        return [piece[None] for piece in pieces]
    groups = [[h * near + f for h in range(facets // near)] for f in range(near)]
    return [lax.all_gather(piece, "facet", axis=0, axis_index_groups=groups) for piece in pieces]


def weight_kernel(
    rows, offset_hbm, owner_hbm, tile_hbm, coord_hbm, fourier_hbm, row_ref, mask_ref, mix_ref, block_ref, *scratch
):
    hbm = (offset_hbm, owner_hbm, tile_hbm, coord_hbm, fourier_hbm)
    offset_ref, owner_ref, tile_ref, coord_ref, sems = scratch
    targets = (*scratch[:4], block_ref)
    copies = [pltpu.make_async_copy(a, b, sems.at[k]) for k, (a, b) in enumerate(zip(hbm, targets))]
    for copy in copies:
        copy.start()
    facets = lax.axis_size("facet")
    band, chan = lax.axis_index("facet"), lax.axis_index("chan")

    for copy in copies[:4]:
        copy.wait()

    blocks = tile_ref.shape[0]
    sublane = lax.broadcasted_iota(jnp.int32, (blocks, LANE), 0)
    lane = lax.broadcasted_iota(jnp.int32, (blocks, LANE), 1)
    tile = jnp.zeros((blocks, LANE), jnp.int32)
    for b in range(blocks):
        tile = jnp.where(sublane == b, tile_ref[b], tile)
    slot = jnp.where(tile < 0, -1, tile // WIN)
    first_row = jnp.zeros((blocks, LANE), jnp.int32)
    seen = jnp.int32(0)
    for pair in range(0, owner_ref.shape[0], LANE // WIN):
        mask = jnp.zeros((blocks, LANE), jnp.float32)
        for k in range(LANE // WIN):
            owned = owner_ref[pair + k] == band
            chosen = slot == jnp.where(owned, seen, -2)
            seen = seen + jnp.where(owned, 1, 0)
            first_row = jnp.where(chosen, offset_ref[1, pair + k], first_row)
            mask = jnp.where(chosen & (lane // WIN == k), 1.0, mask)
        mask_ref[:, pair * WIN : pair * WIN + LANE] = mask

    scale = float((FACET * rows * facets) ** -0.5)
    v = lane % WIN
    up = jnp.maximum(tile, 0) % WIN * v * (SKY // WIN)
    near = SIDE if facets > SIDE else facets
    for h in range(facets // near):
        for r in range(rows):
            position = h % SIDE * FACET + h // SIDE * rows + r
            cosines, sines = turns(up - (first_row + v) * position)
            for part, value in enumerate((cosines, sines)):
                total = jnp.sum(jnp.where(lane < WIN, value, 0.0), axis=1, keepdims=True) * scale
                row_ref[part, h * rows + r] = jnp.broadcast_to(total, (blocks, LANE))

    coord = coord_ref[chan]
    tall = lax.broadcasted_iota(jnp.int32, (2 * rows, LANE), 0)
    for k in range(mix_ref.shape[0]):
        term = 2 * ((chan // 2) ^ k) + tall // rows
        power = jnp.ones((2 * rows, LANE), jnp.float32)
        for degree in range(1, TAYLOR):
            power = jnp.where(term >= degree, power * coord, power)
        mix_ref[k] = power
    copies[4].wait()


def finish_weights(offsets, owner, tiles, coord, fourier, facets, chans, rows):
    subgrids = owner.shape[0]
    blocks = tiles.shape[0]
    near = SIDE if facets > SIDE else facets
    shapes = [
        jax.ShapeDtypeStruct((2, facets // near * rows, blocks, LANE), jnp.float32),
        jax.ShapeDtypeStruct((blocks, subgrids * WIN), jnp.float32),
        jax.ShapeDtypeStruct((chans // 2, 2 * rows, LANE), jnp.float32),
        jax.ShapeDtypeStruct(fourier.shape, jnp.float32),
    ]
    return pl.pallas_call(
        functools.partial(weight_kernel, rows),
        in_specs=[pl.BlockSpec(memory_space=pltpu.HBM)] * 5,
        out_specs=[pl.BlockSpec(memory_space=pltpu.VMEM)] * 4,
        out_shape=shapes,
        scratch_shapes=[
            pltpu.SMEM(offsets.shape, jnp.int32),
            pltpu.SMEM(owner.shape, jnp.int32),
            pltpu.SMEM(tiles.shape, jnp.int32),
            pltpu.SMEM(coord.shape, jnp.float32),
            pltpu.SemaphoreType.DMA((5,)),
        ],
        cost_estimate=lasting(1.3),
        compiler_params=pltpu.CompilerParams(vmem_limit_bytes=grant(*shapes)),
        name="finish_weights",
    )(*(pltpu.with_memory_space_constraint(array, pltpu.HBM) for array in (offsets, owner, tiles, coord, fourier)))


def finish_kernel(pieces, *refs):
    piece_refs = refs[:pieces]
    row_ref, mask_ref, mix_ref, block_ref, out_ref = refs[pieces:]
    groups, tall, width = piece_refs[0].shape
    rows = tall // 2
    subgrids = mask_ref.shape[1] // WIN
    group = math.gcd(subgrids, 4)
    count = group * WIN
    blocks = mask_ref.shape[0]
    real_row = imag_row = 0.0
    for first in range(0, subgrids, group):
        start = 2 * first * WIN
        real_t = imag_t = 0.0
        for h in range(groups):
            mixed = 0.0
            for k in range(pieces):
                weight = jnp.tile(mix_ref[k], (1, 2 * count // LANE))
                mixed = mixed + piece_refs[k][h, :, start : start + 2 * count] * weight
            mixed = mixed[:rows] + mixed[rows:]
            for r in range(rows):
                real_a = jnp.tile(row_ref[0, h * rows + r], (1, count // LANE))
                imag_a = jnp.tile(row_ref[1, h * rows + r], (1, count // LANE))
                real_y, imag_y = mixed[r : r + 1, :count], mixed[r : r + 1, count:]
                real_t = real_t + (real_a * real_y - imag_a * imag_y)
                imag_t = imag_t + (real_a * imag_y + imag_a * real_y)
        mask = mask_ref[:, first * WIN : first * WIN + count]
        for k in range(0, count, LANE):
            real_row = real_row + (real_t * mask)[:, k : k + LANE]
            imag_row = imag_row + (imag_t * mask)[:, k : k + LANE]
    row = jnp.concatenate(
        [sum(value[:, k : k + WIN] for k in range(0, LANE, WIN)) for value in (real_row, imag_row)], axis=1
    )
    high, low = split(row)
    both = jnp.concatenate(
        [jnp.concatenate([high, high], axis=1), jnp.concatenate([low, jnp.zeros_like(low)], axis=1)], axis=0
    )
    here = lax.broadcasted_iota(jnp.int32, (blocks, block_ref.shape[2]), 0)
    dot = functools.partial(jnp.dot, preferred_element_type=jnp.float32)
    total = 0.0
    for b in range(blocks):
        wide = dot(both, block_ref[b])
        total = jnp.where(here == b, wide[:blocks] + wide[blocks:], total)
    for b in range(blocks):
        out_ref[b] = total[b : b + 1]


def finish(pieces, weights, transformed):
    blocks, _, width = transformed.shape
    return pl.pallas_call(
        functools.partial(finish_kernel, len(pieces)),
        in_specs=[pl.BlockSpec(memory_space=pltpu.VMEM)] * (len(pieces) + 4),
        out_specs=pl.BlockSpec(memory_space=pltpu.VMEM),
        out_shape=jax.ShapeDtypeStruct((blocks, 1, width), jnp.float32),
        cost_estimate=lasting(1.3),
        compiler_params=pltpu.CompilerParams(vmem_limit_bytes=grant(*pieces, *weights, transformed)),
        name="finish",
    )(*pieces, *weights, transformed)


def block_kernel(fourier_ref, out_ref):
    vis = out_ref.shape[2] // 2
    here = lax.broadcasted_iota(jnp.int32, (2 * WIN, 2 * WIN), 0)
    there = lax.broadcasted_iota(jnp.int32, (2 * WIN, 2 * WIN), 1)
    cosines, sines = turns((here % WIN) * (there % WIN) * (SKY // WIN))
    sines = jnp.where(here < WIN, -sines, sines)
    table_high, table_low = split(jnp.where((here < WIN) == (there < WIN), cosines, sines) * (1.0 / WIN))
    dot = functools.partial(jnp.dot, preferred_element_type=jnp.float32)
    for b in range(0, out_ref.shape[0], 2):
        pair = [
            jnp.concatenate([fourier_ref[k, 0, :, :vis], fourier_ref[k, 0, :, vis:]], axis=0) for k in (b, b + 1)
        ]
        high, low = split(jnp.concatenate(pair, axis=1))
        done = dot(table_high, high) + (dot(table_low, high) + dot(table_high, low))
        for k in (0, 1):
            real, imag = done[:WIN, k * vis : (k + 1) * vis], done[WIN:, k * vis : (k + 1) * vis]
            matrix = jnp.concatenate(
                [jnp.concatenate([real, imag], axis=1), jnp.concatenate([-imag, real], axis=1)], axis=0
            )
            out_ref[b + k, : 2 * WIN], out_ref[b + k, 2 * WIN :] = split(matrix)


def transform_blocks(fourier):
    blocks, _, _, width = fourier.shape
    vis = width // 2
    return pl.pallas_call(
        block_kernel,
        in_specs=[pl.BlockSpec(memory_space=pltpu.VMEM)],
        out_specs=pl.BlockSpec(memory_space=pltpu.VMEM),
        out_shape=jax.ShapeDtypeStruct((blocks, 4 * WIN, 2 * vis), jnp.bfloat16),
        cost_estimate=lasting(0.7),
        compiler_params=pltpu.CompilerParams(vmem_limit_bytes=grant(fourier, fourier, fourier)),
        name="transform_blocks",
    )(fourier)


def local(taylor, chan_coord, sub_offset, sub_owner, tile_list, fourier):
    facets, chans = lax.axis_size("facet"), lax.axis_size("chan")
    chan = lax.axis_index("chan")
    offsets = sub_offset.T
    beside = exchange(taylor, facets, chans, 0, 1)
    *tables, own = own_columns(offsets, taylor)
    other = column_transform(beside, tables)
    odd = chan % 2 == 1
    both = jnp.concatenate([jnp.where(odd, other, own), jnp.where(odd, own, other)], axis=0)
    *weights, blocks = finish_weights(offsets, sub_owner, tile_list, chan_coord, fourier, facets, chans, taylor.shape[2])
    transformed = transform_blocks(blocks)
    pieces = gather_terms(both, facets, chans)
    return finish(pieces, weights, transformed)


def solution(mesh):
    return jax.shard_map(
        local,
        mesh=mesh,
        in_specs=(
            P("facet", "chan", None, None),
            P(),
            P(),
            P(),
            P("facet"),
            P("facet", "chan", None, None),
        ),
        out_specs=P("facet", "chan", None),
        check_vma=False,
    )
```

```python
import functools
import math

import jax
import jax.numpy as jnp
from jax import lax
from jax.experimental import pallas as pl
from jax.experimental.pallas import tpu as pltpu
from jax.sharding import PartitionSpec as P

FACET = 8192
SIDE = 8
SKY = 65536
WIN = 64
TAYLOR = 4
LANE = 128
BLOCK = 256

SINE = (1.5707963705062866, -0.6459637880325317, 0.07968991994857788, -0.004674150608479977, 0.0001516751217423007)
COSINE = (0.9999999403953552, -1.2336982488632202, 0.2536506950855255, -0.020810570567846298, 0.0008581625297665596)


def turns(index):
    centred = ((index + SKY // 2) & (SKY - 1)) - SKY // 2
    z = centred.astype(jnp.float32) * (2.0 / SKY)
    w = z * z
    half_sin = z * (SINE[0] + w * (SINE[1] + w * (SINE[2] + w * (SINE[3] + w * SINE[4]))))
    half_cos = COSINE[0] + w * (COSINE[1] + w * (COSINE[2] + w * (COSINE[3] + w * COSINE[4])))
    return 1.0 - 2.0 * half_sin * half_sin, 2.0 * half_sin * half_cos


def grant(*arrays):
    return (8 << 20) + 2 * sum(4 * math.prod(array.shape) for array in arrays)


def lasting(microseconds):
    return pl.CostEstimate(flops=int(microseconds * 1.15e9), bytes_accessed=0, transcendentals=0)


def split(value):
    high = value.astype(jnp.bfloat16)
    return high, (value - high.astype(jnp.float32)).astype(jnp.bfloat16)


def rotate(real, imag, cosines, sines):
    return real * cosines + imag * sines, imag * cosines - real * sines


def write_tables(group, step, anchor, offset_ref, look_ref, turn_ref):
    count = group * WIN
    lane_index = lax.broadcasted_iota(jnp.int32, (1, count), 1)
    sublane = lax.broadcasted_iota(jnp.int32, (16, count), 0)
    hops = turn_ref.shape[0] // 2 - step
    shifts = [16, 32, 64] + [BLOCK * step << k for k in range(hops)] + [anchor + k * BLOCK for k in range(step)]
    shift = sum(jnp.where(sublane == k, value, 0) for k, value in enumerate(shifts))
    for first in range(0, offset_ref.shape[1], group):
        freq = lane_index % WIN
        for k in range(group):
            freq = freq + jnp.where(lane_index // WIN == k, offset_ref[0, first + k], 0)
        cosines, sines = turns(shift * freq)
        turned = [(cosines[k : k + 1], sines[k : k + 1]) for k in range(len(shifts))]
        cosines, sines = turns(sublane * freq)
        tables = [(cosines, -sines)]
        for k in range(2):
            tables = tables + [rotate(*table, *turned[k]) for table in tables]
        while len(tables) < BLOCK // 16:
            tables.append(rotate(*tables[-4], *turned[2]))
        for part in (0, 1):
            high, low = split(jnp.concatenate([table[part] for table in tables], axis=0))
            start = (2 * first + part * group) * WIN
            look_ref[0, :, start : start + count] = high
            look_ref[1, :, start : start + count] = low
        for k, hop in enumerate(turned[3:]):
            for part in (0, 1):
                turn_ref[2 * k + part : 2 * k + part + 1, first * WIN : first * WIN + count] = hop[part]


def columns(group, step, term_ref, look_ref, turn_ref):
    rows, width = term_ref.shape[2:]
    count = group * WIN
    tall = step * rows
    hops = turn_ref.shape[0] // 2 - step
    folded = jnp.concatenate([term_ref[0, 0, :, k * BLOCK : (k + 1) * BLOCK] for k in range(width // BLOCK)], axis=0)
    term_high, term_low = split(folded)
    dot = functools.partial(jnp.dot, preferred_element_type=jnp.float32)
    for first in range(0, turn_ref.shape[1] // WIN, group):
        start = 2 * first * WIN
        look_high = look_ref[0, :, start : start + 2 * count]
        look_low = look_ref[1, :, start : start + 2 * count]
        part = dot(term_high, look_high) + (dot(term_low, look_high) + dot(term_high, look_low))
        turn = [turn_ref[k : k + 1, first * WIN : first * WIN + count] for k in range(turn_ref.shape[0])]
        pieces = []
        for k in range(0, part.shape[0], tall):
            pieces.append((part[k : k + tall, :count], part[k : k + tall, count:]))
        for k in range(hops):
            merged = []
            for near, far in zip(pieces[::2], pieces[1::2]):
                moved = rotate(*far, turn[2 * k], turn[2 * k + 1])
                merged.append((near[0] + moved[0], near[1] + moved[1]))
            pieces = merged
        (real, imag), = pieces
        total_real = total_imag = 0.0
        for k in range(step):
            mine = slice(k * rows, (k + 1) * rows)
            piece = rotate(real[mine], imag[mine], turn[2 * (hops + k)], turn[2 * (hops + k) + 1])
            total_real, total_imag = total_real + piece[0], total_imag + piece[1]
        yield start, count, total_real, total_imag


def own_kernel(group, step, offset_hbm, term_hbm, look_ref, turn_ref, out_ref, *scratch):
    offset_ref, term_ref, sems = scratch
    moves = ((offset_hbm, offset_ref), (term_hbm, term_ref))
    copies = [pltpu.make_async_copy(a, b, sems.at[k]) for k, (a, b) in enumerate(moves)]
    for copy in copies:
        copy.start()
    anchor = lax.axis_index("facet") % SIDE * FACET
    copies[0].wait()
    write_tables(group, step, anchor, offset_ref, look_ref, turn_ref)
    copies[1].wait()
    for start, count, real, imag in columns(group, step, term_ref, look_ref, turn_ref):
        out_ref[:, start : start + count] = real
        out_ref[:, start + count : start + 2 * count] = imag


def other_kernel(group, step, term_ref, look_ref, turn_ref, own_ref, out_ref):
    rows = own_ref.shape[0]
    odd = lax.axis_index("chan") % 2 == 1
    for start, count, *other in columns(group, step, term_ref, look_ref, turn_ref):
        for k, value in enumerate(other):
            place = slice(start + k * count, start + (k + 1) * count)
            own = own_ref[:, place]
            out_ref[:rows, place] = jnp.where(odd, value, own)
            out_ref[rows:, place] = jnp.where(odd, own, value)


def own_columns(offsets, taylor):
    rows, width = taylor.shape[2:]
    subgrids = offsets.shape[1]
    step = max(8 // rows, 1)
    hops = (width // BLOCK // step).bit_length() - 1
    shapes = [
        jax.ShapeDtypeStruct((2, BLOCK, 2 * subgrids * WIN), jnp.bfloat16),
        jax.ShapeDtypeStruct((2 * (hops + step), subgrids * WIN), jnp.float32),
        jax.ShapeDtypeStruct((rows, 2 * subgrids * WIN), jnp.float32),
    ]
    return pl.pallas_call(
        functools.partial(own_kernel, math.gcd(subgrids, 4), step),
        in_specs=[pl.BlockSpec(memory_space=pltpu.HBM)] * 2,
        out_specs=[pl.BlockSpec(memory_space=pltpu.VMEM)] * 3,
        out_shape=shapes,
        scratch_shapes=[
            pltpu.SMEM(offsets.shape, jnp.int32),
            pltpu.VMEM(taylor.shape, jnp.float32),
            pltpu.SemaphoreType.DMA((2,)),
        ],
        cost_estimate=lasting(1.4),
        compiler_params=pltpu.CompilerParams(vmem_limit_bytes=grant(*shapes)),
        name="own_columns",
    )(*(pltpu.with_memory_space_constraint(array, pltpu.HBM) for array in (offsets, taylor)))


def both_columns(taylor, tables, own):
    rows = taylor.shape[2]
    columns_out = tables[0].shape[2]
    return pl.pallas_call(
        functools.partial(other_kernel, math.gcd(columns_out // (2 * WIN), 4), max(8 // rows, 1)),
        in_specs=[pl.BlockSpec(memory_space=pltpu.VMEM)] * 4,
        out_specs=pl.BlockSpec(memory_space=pltpu.VMEM),
        out_shape=jax.ShapeDtypeStruct((2 * rows, columns_out), jnp.float32),
        cost_estimate=lasting(0.35),
        compiler_params=pltpu.CompilerParams(vmem_limit_bytes=grant(taylor, *tables)),
        name="both_columns",
    )(taylor, *tables, own)


def exchange(value, facets, chans, flip_facet, flip_chan):
    pairs = [
        (f * chans + c, (f ^ flip_facet) * chans + (c ^ flip_chan)) for f in range(facets) for c in range(chans)
    ]
    return lax.ppermute(value, ("facet", "chan"), pairs)


def gather_terms(both, facets, chans):
    near = SIDE if facets > SIDE else facets
    step = 1
    while step < near:
        both = both + exchange(both, facets, chans, step, 1)
        step *= 2
    pieces = [both]
    step = 2
    while step < chans:
        pieces = pieces + [exchange(piece, facets, chans, 0, step + 1) for piece in pieces]
        step *= 2
    if facets == near:
        return [piece[None] for piece in pieces]
    groups = [[h * near + f for h in range(facets // near)] for f in range(near)]
    return [lax.all_gather(piece, "facet", axis=0, axis_index_groups=groups) for piece in pieces]


def weight_kernel(
    rows, offset_hbm, owner_hbm, tile_hbm, coord_hbm, fourier_hbm, row_ref, mask_ref, mix_ref, block_ref, *scratch
):
    hbm = (offset_hbm, owner_hbm, tile_hbm, coord_hbm, fourier_hbm)
    offset_ref, owner_ref, tile_ref, coord_ref, sems = scratch
    targets = (*scratch[:4], block_ref)
    copies = [pltpu.make_async_copy(a, b, sems.at[k]) for k, (a, b) in enumerate(zip(hbm, targets))]
    for copy in copies:
        copy.start()
    facets = lax.axis_size("facet")
    band, chan = lax.axis_index("facet"), lax.axis_index("chan")

    for copy in copies[:4]:
        copy.wait()

    blocks = tile_ref.shape[0]
    sublane = lax.broadcasted_iota(jnp.int32, (blocks, LANE), 0)
    lane = lax.broadcasted_iota(jnp.int32, (blocks, LANE), 1)
    tile = jnp.zeros((blocks, LANE), jnp.int32)
    for b in range(blocks):
        tile = jnp.where(sublane == b, tile_ref[b], tile)
    slot = jnp.where(tile < 0, -1, tile // WIN)
    first_row = jnp.zeros((blocks, LANE), jnp.int32)
    seen = jnp.int32(0)
    for pair in range(0, owner_ref.shape[0], LANE // WIN):
        mask = jnp.zeros((blocks, LANE), jnp.float32)
        for k in range(LANE // WIN):
            owned = owner_ref[pair + k] == band
            chosen = slot == jnp.where(owned, seen, -2)
            seen = seen + jnp.where(owned, 1, 0)
            first_row = jnp.where(chosen, offset_ref[1, pair + k], first_row)
            mask = jnp.where(chosen & (lane // WIN == k), 1.0, mask)
        mask_ref[:, pair * WIN : pair * WIN + LANE] = mask

    scale = float((FACET * rows * facets) ** -0.5)
    v = lane % WIN
    up = jnp.maximum(tile, 0) % WIN * v * (SKY // WIN)
    near = SIDE if facets > SIDE else facets
    for h in range(facets // near):
        for r in range(rows):
            position = h % SIDE * FACET + h // SIDE * rows + r
            cosines, sines = turns(up - (first_row + v) * position)
            for part, value in enumerate((cosines, sines)):
                total = jnp.sum(jnp.where(lane < WIN, value, 0.0), axis=1, keepdims=True) * scale
                row_ref[part, h * rows + r] = jnp.broadcast_to(total, (blocks, LANE))

    coord = coord_ref[chan]
    tall = lax.broadcasted_iota(jnp.int32, (2 * rows, LANE), 0)
    for k in range(mix_ref.shape[0]):
        term = 2 * ((chan // 2) ^ k) + tall // rows
        power = jnp.ones((2 * rows, LANE), jnp.float32)
        for degree in range(1, TAYLOR):
            power = jnp.where(term >= degree, power * coord, power)
        mix_ref[k] = power
    copies[4].wait()


def finish_weights(offsets, owner, tiles, coord, fourier, facets, chans, rows):
    subgrids = owner.shape[0]
    blocks = tiles.shape[0]
    near = SIDE if facets > SIDE else facets
    shapes = [
        jax.ShapeDtypeStruct((2, facets // near * rows, blocks, LANE), jnp.float32),
        jax.ShapeDtypeStruct((blocks, subgrids * WIN), jnp.float32),
        jax.ShapeDtypeStruct((chans // 2, 2 * rows, LANE), jnp.float32),
        jax.ShapeDtypeStruct(fourier.shape, jnp.float32),
    ]
    return pl.pallas_call(
        functools.partial(weight_kernel, rows),
        in_specs=[pl.BlockSpec(memory_space=pltpu.HBM)] * 5,
        out_specs=[pl.BlockSpec(memory_space=pltpu.VMEM)] * 4,
        out_shape=shapes,
        scratch_shapes=[
            pltpu.SMEM(offsets.shape, jnp.int32),
            pltpu.SMEM(owner.shape, jnp.int32),
            pltpu.SMEM(tiles.shape, jnp.int32),
            pltpu.SMEM(coord.shape, jnp.float32),
            pltpu.SemaphoreType.DMA((5,)),
        ],
        cost_estimate=lasting(1.3),
        compiler_params=pltpu.CompilerParams(vmem_limit_bytes=grant(*shapes)),
        name="finish_weights",
    )(*(pltpu.with_memory_space_constraint(array, pltpu.HBM) for array in (offsets, owner, tiles, coord, fourier)))


def finish_kernel(pieces, *refs):
    piece_refs = refs[:pieces]
    row_ref, mask_ref, mix_ref, block_ref, out_ref = refs[pieces:]
    groups, tall, width = piece_refs[0].shape
    rows = tall // 2
    subgrids = mask_ref.shape[1] // WIN
    group = math.gcd(subgrids, 4)
    count = group * WIN
    blocks = mask_ref.shape[0]
    real_row = imag_row = 0.0
    for first in range(0, subgrids, group):
        start = 2 * first * WIN
        real_t = imag_t = 0.0
        for h in range(groups):
            mixed = 0.0
            for k in range(pieces):
                weight = jnp.tile(mix_ref[k], (1, 2 * count // LANE))
                mixed = mixed + piece_refs[k][h, :, start : start + 2 * count] * weight
            mixed = mixed[:rows] + mixed[rows:]
            for r in range(rows):
                real_a = jnp.tile(row_ref[0, h * rows + r], (1, count // LANE))
                imag_a = jnp.tile(row_ref[1, h * rows + r], (1, count // LANE))
                real_y, imag_y = mixed[r : r + 1, :count], mixed[r : r + 1, count:]
                real_t = real_t + (real_a * real_y - imag_a * imag_y)
                imag_t = imag_t + (real_a * imag_y + imag_a * real_y)
        mask = mask_ref[:, first * WIN : first * WIN + count]
        for k in range(0, count, LANE):
            real_row = real_row + (real_t * mask)[:, k : k + LANE]
            imag_row = imag_row + (imag_t * mask)[:, k : k + LANE]
    row = jnp.concatenate(
        [sum(value[:, k : k + WIN] for k in range(0, LANE, WIN)) for value in (real_row, imag_row)], axis=1
    )
    none = jnp.zeros((8, WIN), jnp.float32)
    odd = lax.broadcasted_iota(jnp.int32, (8, 4 * WIN), 0) % 2 == 1
    here = lax.broadcasted_iota(jnp.int32, (8, block_ref.shape[2]), 0) // 2
    vis = block_ref.shape[2] // 2
    for first in range(0, blocks, 8):
        mine = row[first : first + 8]
        high = mine.astype(jnp.bfloat16).astype(jnp.float32)
        sides = []
        for value, again in ((high, True), (mine - high, False)):
            for part in (value[:, :WIN], value[:, WIN:]):
                wide = [part, part if again else none]
                even_side, odd_side = jnp.concatenate([*wide, none, none], axis=1), jnp.concatenate([none, none, *wide], axis=1)
                sides.append(jnp.where(odd, odd_side, even_side))
        left = jnp.concatenate(sides, axis=0).astype(jnp.bfloat16)
        real_c, imag_c = 0.0, 0.0
        for b in range(4):
            wide = jnp.dot(left, block_ref[first // 2 + b], preferred_element_type=jnp.float32)
            real_c = jnp.where(here == b, wide[:8] + wide[16:24], real_c)
            imag_c = jnp.where(here == b, wide[8:16] + wide[24:], imag_c)
        real_v, imag_v = real_c[:, :vis] - imag_c[:, vis:], real_c[:, vis:] + imag_c[:, :vis]
        for b in range(8):
            out_ref[first + b, :, :vis] = real_v[b : b + 1]
            out_ref[first + b, :, vis:] = imag_v[b : b + 1]


def finish(pieces, weights, transformed):
    blocks, width = 2 * transformed.shape[0], transformed.shape[2]
    return pl.pallas_call(
        functools.partial(finish_kernel, len(pieces)),
        in_specs=[pl.BlockSpec(memory_space=pltpu.VMEM)] * (len(pieces) + 4),
        out_specs=pl.BlockSpec(memory_space=pltpu.VMEM),
        out_shape=jax.ShapeDtypeStruct((blocks, 1, width), jnp.float32),
        cost_estimate=lasting(1.3),
        compiler_params=pltpu.CompilerParams(vmem_limit_bytes=grant(*pieces, *weights, transformed)),
        name="finish",
    )(*pieces, *weights, transformed)


def block_kernel(fourier_ref, out_ref):
    vis = out_ref.shape[2] // 2
    here = lax.broadcasted_iota(jnp.int32, (2 * WIN, 2 * WIN), 0)
    there = lax.broadcasted_iota(jnp.int32, (2 * WIN, 2 * WIN), 1)
    cosines, sines = turns((here % WIN) * (there % WIN) * (SKY // WIN))
    sines = jnp.where(here < WIN, -sines, sines)
    table_high, table_low = split(jnp.where((here < WIN) == (there < WIN), cosines, sines) * (1.0 / WIN))
    dot = functools.partial(jnp.dot, preferred_element_type=jnp.float32)
    for b in range(0, fourier_ref.shape[0], 2):
        pair = [
            jnp.concatenate([fourier_ref[k, 0, :, :vis], fourier_ref[k, 0, :, vis:]], axis=0) for k in (b, b + 1)
        ]
        high, low = split(jnp.concatenate(pair, axis=1))
        done = dot(table_high, high) + (dot(table_low, high) + dot(table_high, low))
        for k in (0, 1):
            matrix = jnp.concatenate([done[:WIN, k * vis : (k + 1) * vis], done[WIN:, k * vis : (k + 1) * vis]], axis=1)
            start = 2 * WIN * k
            out_ref[b // 2, start : start + WIN], out_ref[b // 2, start + WIN : start + 2 * WIN] = split(matrix)


def transform_blocks(fourier):
    blocks, _, _, width = fourier.shape
    vis = width // 2
    return pl.pallas_call(
        block_kernel,
        in_specs=[pl.BlockSpec(memory_space=pltpu.VMEM)],
        out_specs=pl.BlockSpec(memory_space=pltpu.VMEM),
        out_shape=jax.ShapeDtypeStruct((blocks // 2, 4 * WIN, 2 * vis), jnp.bfloat16),
        cost_estimate=lasting(0.7),
        compiler_params=pltpu.CompilerParams(vmem_limit_bytes=grant(fourier, fourier, fourier)),
        name="transform_blocks",
    )(fourier)


def local(taylor, chan_coord, sub_offset, sub_owner, tile_list, fourier):
    facets, chans = lax.axis_size("facet"), lax.axis_size("chan")
    offsets = sub_offset.T
    beside = exchange(taylor, facets, chans, 0, 1)
    *tables, own = own_columns(offsets, taylor)
    both = both_columns(beside, tables, own)
    *weights, blocks = finish_weights(offsets, sub_owner, tile_list, chan_coord, fourier, facets, chans, taylor.shape[2])
    transformed = transform_blocks(blocks)
    pieces = gather_terms(both, facets, chans)
    return finish(pieces, weights, transformed)


def solution(mesh):
    return jax.shard_map(
        local,
        mesh=mesh,
        in_specs=(
            P("facet", "chan", None, None),
            P(),
            P(),
            P(),
            P("facet"),
            P("facet", "chan", None, None),
        ),
        out_specs=P("facet", "chan", None),
        check_vma=False,
    )
```

```python
import functools
import math

import jax
import jax.numpy as jnp
from jax import lax
from jax.experimental import pallas as pl
from jax.experimental.pallas import tpu as pltpu
from jax.sharding import PartitionSpec as P

FACET = 8192
SIDE = 8
SKY = 65536
WIN = 64
TAYLOR = 4
LANE = 128
BLOCK = 256

SINE = (1.5707963705062866, -0.6459637880325317, 0.07968991994857788, -0.004674150608479977, 0.0001516751217423007)
COSINE = (0.9999999403953552, -1.2336982488632202, 0.2536506950855255, -0.020810570567846298, 0.0008581625297665596)


def turns(index):
    centred = ((index + SKY // 2) & (SKY - 1)) - SKY // 2
    z = centred.astype(jnp.float32) * (2.0 / SKY)
    w = z * z
    half_sin = z * (SINE[0] + w * (SINE[1] + w * (SINE[2] + w * (SINE[3] + w * SINE[4]))))
    half_cos = COSINE[0] + w * (COSINE[1] + w * (COSINE[2] + w * (COSINE[3] + w * COSINE[4])))
    return 1.0 - 2.0 * half_sin * half_sin, 2.0 * half_sin * half_cos


def grant(*arrays):
    return (8 << 20) + 2 * sum(4 * math.prod(array.shape) for array in arrays)


def lasting(microseconds):
    return pl.CostEstimate(flops=int(microseconds * 1.15e9), bytes_accessed=0, transcendentals=0)


def split(value):
    high = value.astype(jnp.bfloat16)
    return high, (value - high.astype(jnp.float32)).astype(jnp.bfloat16)


def rotate(real, imag, cosines, sines):
    return real * cosines + imag * sines, imag * cosines - real * sines


def write_tables(group, step, anchor, offset_ref, look_ref, turn_ref):
    count = group * WIN
    lane_index = lax.broadcasted_iota(jnp.int32, (1, count), 1)
    sublane = lax.broadcasted_iota(jnp.int32, (16, count), 0)
    hops = turn_ref.shape[0] // 2 - step
    shifts = [16, 32, 64] + [BLOCK * step << k for k in range(hops)] + [anchor + k * BLOCK for k in range(step)]
    shift = sum(jnp.where(sublane == k, value, 0) for k, value in enumerate(shifts))
    for first in range(0, offset_ref.shape[1], group):
        freq = lane_index % WIN
        for k in range(group):
            freq = freq + jnp.where(lane_index // WIN == k, offset_ref[0, first + k], 0)
        cosines, sines = turns(shift * freq)
        turned = [(cosines[k : k + 1], sines[k : k + 1]) for k in range(len(shifts))]
        cosines, sines = turns(sublane * freq)
        tables = [(cosines, -sines)]
        for k in range(2):
            tables = tables + [rotate(*table, *turned[k]) for table in tables]
        while len(tables) < BLOCK // 16:
            tables.append(rotate(*tables[-4], *turned[2]))
        for part in (0, 1):
            high, low = split(jnp.concatenate([table[part] for table in tables], axis=0))
            start = (2 * first + part * group) * WIN
            look_ref[0, :, start : start + count] = high
            look_ref[1, :, start : start + count] = low
        for k, hop in enumerate(turned[3:]):
            for part in (0, 1):
                turn_ref[2 * k + part : 2 * k + part + 1, first * WIN : first * WIN + count] = hop[part]


def columns(group, step, term_ref, look_ref, turn_ref):
    rows, width = term_ref.shape[2:]
    count = group * WIN
    tall = step * rows
    hops = turn_ref.shape[0] // 2 - step
    folded = jnp.concatenate([term_ref[0, 0, :, k * BLOCK : (k + 1) * BLOCK] for k in range(width // BLOCK)], axis=0)
    term_high, term_low = split(folded)
    dot = functools.partial(jnp.dot, preferred_element_type=jnp.float32)
    for first in range(0, turn_ref.shape[1] // WIN, group):
        start = 2 * first * WIN
        look_high = look_ref[0, :, start : start + 2 * count]
        look_low = look_ref[1, :, start : start + 2 * count]
        part = dot(term_high, look_high) + (dot(term_low, look_high) + dot(term_high, look_low))
        turn = [turn_ref[k : k + 1, first * WIN : first * WIN + count] for k in range(turn_ref.shape[0])]
        pieces = []
        for k in range(0, part.shape[0], tall):
            pieces.append((part[k : k + tall, :count], part[k : k + tall, count:]))
        for k in range(hops):
            merged = []
            for near, far in zip(pieces[::2], pieces[1::2]):
                moved = rotate(*far, turn[2 * k], turn[2 * k + 1])
                merged.append((near[0] + moved[0], near[1] + moved[1]))
            pieces = merged
        (real, imag), = pieces
        total_real = total_imag = 0.0
        for k in range(step):
            mine = slice(k * rows, (k + 1) * rows)
            piece = rotate(real[mine], imag[mine], turn[2 * (hops + k)], turn[2 * (hops + k) + 1])
            total_real, total_imag = total_real + piece[0], total_imag + piece[1]
        yield start, count, total_real, total_imag


def own_kernel(group, step, offset_hbm, term_hbm, look_ref, turn_ref, out_ref, *scratch):
    offset_ref, term_ref, sems = scratch
    moves = ((offset_hbm, offset_ref), (term_hbm, term_ref))
    copies = [pltpu.make_async_copy(a, b, sems.at[k]) for k, (a, b) in enumerate(moves)]
    for copy in copies:
        copy.start()
    anchor = lax.axis_index("facet") % SIDE * FACET
    copies[0].wait()
    write_tables(group, step, anchor, offset_ref, look_ref, turn_ref)
    copies[1].wait()
    for start, count, real, imag in columns(group, step, term_ref, look_ref, turn_ref):
        out_ref[:, start : start + count] = real
        out_ref[:, start + count : start + 2 * count] = imag


def other_kernel(group, step, term_ref, look_ref, turn_ref, own_ref, out_ref):
    rows = own_ref.shape[0]
    odd = lax.axis_index("chan") % 2 == 1
    for start, count, *other in columns(group, step, term_ref, look_ref, turn_ref):
        for k, value in enumerate(other):
            place = slice(start + k * count, start + (k + 1) * count)
            own = own_ref[:, place]
            out_ref[:rows, place] = jnp.where(odd, value, own)
            out_ref[rows:, place] = jnp.where(odd, own, value)


def own_columns(offsets, taylor):
    rows, width = taylor.shape[2:]
    subgrids = offsets.shape[1]
    step = max(8 // rows, 1)
    hops = (width // BLOCK // step).bit_length() - 1
    shapes = [
        jax.ShapeDtypeStruct((2, BLOCK, 2 * subgrids * WIN), jnp.bfloat16),
        jax.ShapeDtypeStruct((2 * (hops + step), subgrids * WIN), jnp.float32),
        jax.ShapeDtypeStruct((rows, 2 * subgrids * WIN), jnp.float32),
    ]
    return pl.pallas_call(
        functools.partial(own_kernel, math.gcd(subgrids, 4), step),
        in_specs=[pl.BlockSpec(memory_space=pltpu.HBM)] * 2,
        out_specs=[pl.BlockSpec(memory_space=pltpu.VMEM)] * 3,
        out_shape=shapes,
        scratch_shapes=[
            pltpu.SMEM(offsets.shape, jnp.int32),
            pltpu.VMEM(taylor.shape, jnp.float32),
            pltpu.SemaphoreType.DMA((2,)),
        ],
        cost_estimate=lasting(1.4),
        compiler_params=pltpu.CompilerParams(vmem_limit_bytes=grant(*shapes)),
        name="own_columns",
    )(*(pltpu.with_memory_space_constraint(array, pltpu.HBM) for array in (offsets, taylor)))


def both_columns(taylor, tables, own):
    rows = taylor.shape[2]
    columns_out = tables[0].shape[2]
    return pl.pallas_call(
        functools.partial(other_kernel, math.gcd(columns_out // (2 * WIN), 4), max(8 // rows, 1)),
        in_specs=[pl.BlockSpec(memory_space=pltpu.VMEM)] * 4,
        out_specs=pl.BlockSpec(memory_space=pltpu.VMEM),
        out_shape=jax.ShapeDtypeStruct((2 * rows, columns_out), jnp.float32),
        cost_estimate=lasting(0.35),
        compiler_params=pltpu.CompilerParams(vmem_limit_bytes=grant(taylor, *tables)),
        name="both_columns",
    )(taylor, *tables, own)


def exchange(value, facets, chans, flip_facet, flip_chan):
    pairs = [
        (f * chans + c, (f ^ flip_facet) * chans + (c ^ flip_chan)) for f in range(facets) for c in range(chans)
    ]
    return lax.ppermute(value, ("facet", "chan"), pairs)


def gather_terms(both, facets, chans):
    near = SIDE if facets > SIDE else facets
    step = 1
    while step < near:
        both = both + exchange(both, facets, chans, step, 1)
        step *= 2
    pieces = [both]
    step = 2
    while step < chans:
        pieces = pieces + [exchange(piece, facets, chans, 0, step + 1) for piece in pieces]
        step *= 2
    if facets == near:
        return [piece[None] for piece in pieces]
    groups = [[h * near + f for h in range(facets // near)] for f in range(near)]
    return [lax.all_gather(piece, "facet", axis=0, axis_index_groups=groups) for piece in pieces]


def weight_kernel(
    rows, offset_hbm, owner_hbm, tile_hbm, coord_hbm, fourier_hbm, row_ref, mask_ref, mix_ref, block_ref, *scratch
):
    hbm = (offset_hbm, owner_hbm, tile_hbm, coord_hbm, fourier_hbm)
    offset_ref, owner_ref, tile_ref, coord_ref, sems = scratch
    targets = (*scratch[:4], block_ref)
    copies = [pltpu.make_async_copy(a, b, sems.at[k]) for k, (a, b) in enumerate(zip(hbm, targets))]
    for copy in copies:
        copy.start()
    facets = lax.axis_size("facet")
    band, chan = lax.axis_index("facet"), lax.axis_index("chan")

    for copy in copies[:4]:
        copy.wait()

    blocks = tile_ref.shape[0]
    sublane = lax.broadcasted_iota(jnp.int32, (blocks, LANE), 0)
    lane = lax.broadcasted_iota(jnp.int32, (blocks, LANE), 1)
    tile = jnp.zeros((blocks, LANE), jnp.int32)
    for b in range(blocks):
        tile = jnp.where(sublane == b, tile_ref[b], tile)
    slot = jnp.where(tile < 0, -1, tile // WIN)
    first_row = jnp.zeros((blocks, LANE), jnp.int32)
    seen = jnp.int32(0)
    for pair in range(0, owner_ref.shape[0], LANE // WIN):
        mask = jnp.zeros((blocks, LANE), jnp.float32)
        for k in range(LANE // WIN):
            owned = owner_ref[pair + k] == band
            chosen = slot == jnp.where(owned, seen, -2)
            seen = seen + jnp.where(owned, 1, 0)
            first_row = jnp.where(chosen, offset_ref[1, pair + k], first_row)
            mask = jnp.where(chosen & (lane // WIN == k), 1.0, mask)
        mask_ref[:, pair * WIN : pair * WIN + LANE] = mask

    scale = float((FACET * rows * facets) ** -0.5)
    v = lane % WIN
    up = jnp.maximum(tile, 0) % WIN * v * (SKY // WIN)
    near = SIDE if facets > SIDE else facets
    for h in range(facets // near):
        for r in range(rows):
            position = h % SIDE * FACET + h // SIDE * rows + r
            cosines, sines = turns(up - (first_row + v) * position)
            for part, value in enumerate((cosines, sines)):
                total = jnp.sum(jnp.where(lane < WIN, value, 0.0), axis=1, keepdims=True) * scale
                row_ref[part, h * rows + r] = jnp.broadcast_to(total, (blocks, LANE))

    coord = coord_ref[chan]
    tall = lax.broadcasted_iota(jnp.int32, (2 * rows, LANE), 0)
    for k in range(mix_ref.shape[0]):
        term = 2 * ((chan // 2) ^ k) + tall // rows
        power = jnp.ones((2 * rows, LANE), jnp.float32)
        for degree in range(1, TAYLOR):
            power = jnp.where(term >= degree, power * coord, power)
        mix_ref[k] = power
    copies[4].wait()


def finish_weights(offsets, owner, tiles, coord, fourier, facets, chans, rows):
    subgrids = owner.shape[0]
    blocks = tiles.shape[0]
    near = SIDE if facets > SIDE else facets
    shapes = [
        jax.ShapeDtypeStruct((2, facets // near * rows, blocks, LANE), jnp.float32),
        jax.ShapeDtypeStruct((blocks, subgrids * WIN), jnp.float32),
        jax.ShapeDtypeStruct((chans // 2, 2 * rows, LANE), jnp.float32),
        jax.ShapeDtypeStruct(fourier.shape, jnp.float32),
    ]
    return pl.pallas_call(
        functools.partial(weight_kernel, rows),
        in_specs=[pl.BlockSpec(memory_space=pltpu.HBM)] * 5,
        out_specs=[pl.BlockSpec(memory_space=pltpu.VMEM)] * 4,
        out_shape=shapes,
        scratch_shapes=[
            pltpu.SMEM(offsets.shape, jnp.int32),
            pltpu.SMEM(owner.shape, jnp.int32),
            pltpu.SMEM(tiles.shape, jnp.int32),
            pltpu.SMEM(coord.shape, jnp.float32),
            pltpu.SemaphoreType.DMA((5,)),
        ],
        cost_estimate=lasting(1.3),
        compiler_params=pltpu.CompilerParams(vmem_limit_bytes=grant(*shapes)),
        name="finish_weights",
    )(*(pltpu.with_memory_space_constraint(array, pltpu.HBM) for array in (offsets, owner, tiles, coord, fourier)))


def finish_kernel(pieces, *refs):
    piece_refs = refs[:pieces]
    row_ref, mask_ref, mix_ref, block_ref, out_ref = refs[pieces:]
    groups, tall, width = piece_refs[0].shape
    rows = tall // 2
    subgrids = mask_ref.shape[1] // WIN
    group = math.gcd(subgrids, 4)
    count = group * WIN
    blocks = mask_ref.shape[0]
    real_row = imag_row = 0.0
    for first in range(0, subgrids, group):
        start = 2 * first * WIN
        real_t = imag_t = 0.0
        for h in range(groups):
            mixed = 0.0
            for k in range(pieces):
                weight = jnp.tile(mix_ref[k], (1, 2 * count // LANE))
                mixed = mixed + piece_refs[k][h, :, start : start + 2 * count] * weight
            mixed = mixed[:rows] + mixed[rows:]
            for r in range(rows):
                real_a = jnp.tile(row_ref[0, h * rows + r], (1, count // LANE))
                imag_a = jnp.tile(row_ref[1, h * rows + r], (1, count // LANE))
                real_y, imag_y = mixed[r : r + 1, :count], mixed[r : r + 1, count:]
                real_t = real_t + (real_a * real_y - imag_a * imag_y)
                imag_t = imag_t + (real_a * imag_y + imag_a * real_y)
        mask = mask_ref[:, first * WIN : first * WIN + count]
        for k in range(0, count, LANE):
            real_row = real_row + (real_t * mask)[:, k : k + LANE]
            imag_row = imag_row + (imag_t * mask)[:, k : k + LANE]
    real_row, imag_row = (sum(pltpu.roll(value, k, 1) for k in range(0, LANE, WIN)) for value in (real_row, imag_row))
    lane = lax.broadcasted_iota(jnp.int32, (8, LANE), 1)
    keep = lane // WIN == lax.broadcasted_iota(jnp.int32, (8, LANE), 0) % 2
    here = lax.broadcasted_iota(jnp.int32, (8, block_ref.shape[2]), 0) // 2
    vis = block_ref.shape[2] // 2
    for first in range(0, blocks, 8):
        highs, lows = [], []
        for value in (real_row, imag_row):
            mine = jnp.where(keep, value[first : first + 8], 0.0)
            high = mine.astype(jnp.bfloat16).astype(jnp.float32)
            highs.append(jnp.concatenate([high, high], axis=1))
            lows.append(jnp.concatenate([mine - high, jnp.zeros_like(mine)], axis=1))
        left = jnp.concatenate(highs + lows, axis=0).astype(jnp.bfloat16)
        real_c, imag_c = 0.0, 0.0
        for b in range(4):
            wide = jnp.dot(left, block_ref[first // 2 + b], preferred_element_type=jnp.float32)
            real_c = jnp.where(here == b, wide[:8] + wide[16:24], real_c)
            imag_c = jnp.where(here == b, wide[8:16] + wide[24:], imag_c)
        real_v, imag_v = real_c[:, :vis] - imag_c[:, vis:], real_c[:, vis:] + imag_c[:, :vis]
        for b in range(8):
            out_ref[first + b, :, :vis] = real_v[b : b + 1]
            out_ref[first + b, :, vis:] = imag_v[b : b + 1]


def finish(pieces, weights, transformed):
    blocks, width = 2 * transformed.shape[0], transformed.shape[2]
    return pl.pallas_call(
        functools.partial(finish_kernel, len(pieces)),
        in_specs=[pl.BlockSpec(memory_space=pltpu.VMEM)] * (len(pieces) + 4),
        out_specs=pl.BlockSpec(memory_space=pltpu.VMEM),
        out_shape=jax.ShapeDtypeStruct((blocks, 1, width), jnp.float32),
        cost_estimate=lasting(1.3),
        compiler_params=pltpu.CompilerParams(vmem_limit_bytes=grant(*pieces, *weights, transformed)),
        name="finish",
    )(*pieces, *weights, transformed)


def block_kernel(fourier_ref, out_ref):
    vis = out_ref.shape[2] // 2
    here = lax.broadcasted_iota(jnp.int32, (2 * WIN, 2 * WIN), 0)
    there = lax.broadcasted_iota(jnp.int32, (2 * WIN, 2 * WIN), 1)
    cosines, sines = turns((here % WIN) * (there % WIN) * (SKY // WIN))
    sines = jnp.where(here < WIN, -sines, sines)
    table_high, table_low = split(jnp.where((here < WIN) == (there < WIN), cosines, sines) * (1.0 / WIN))
    dot = functools.partial(jnp.dot, preferred_element_type=jnp.float32)
    for b in range(0, fourier_ref.shape[0], 2):
        pair = [
            jnp.concatenate([fourier_ref[k, 0, :, :vis], fourier_ref[k, 0, :, vis:]], axis=0) for k in (b, b + 1)
        ]
        high, low = split(jnp.concatenate(pair, axis=1))
        done = dot(table_high, high) + (dot(table_low, high) + dot(table_high, low))
        for k in (0, 1):
            matrix = jnp.concatenate([done[:WIN, k * vis : (k + 1) * vis], done[WIN:, k * vis : (k + 1) * vis]], axis=1)
            high, low = split(matrix)
            out_ref[b // 2, WIN * k : WIN * (k + 1)] = high
            out_ref[b // 2, WIN * (k + 2) : WIN * (k + 3)] = low


def transform_blocks(fourier):
    blocks, _, _, width = fourier.shape
    vis = width // 2
    return pl.pallas_call(
        block_kernel,
        in_specs=[pl.BlockSpec(memory_space=pltpu.VMEM)],
        out_specs=pl.BlockSpec(memory_space=pltpu.VMEM),
        out_shape=jax.ShapeDtypeStruct((blocks // 2, 4 * WIN, 2 * vis), jnp.bfloat16),
        cost_estimate=lasting(0.7),
        compiler_params=pltpu.CompilerParams(vmem_limit_bytes=grant(fourier, fourier, fourier)),
        name="transform_blocks",
    )(fourier)


def local(taylor, chan_coord, sub_offset, sub_owner, tile_list, fourier):
    facets, chans = lax.axis_size("facet"), lax.axis_size("chan")
    offsets = sub_offset.T
    beside = exchange(taylor, facets, chans, 0, 1)
    *tables, own = own_columns(offsets, taylor)
    both = both_columns(beside, tables, own)
    *weights, blocks = finish_weights(offsets, sub_owner, tile_list, chan_coord, fourier, facets, chans, taylor.shape[2])
    transformed = transform_blocks(blocks)
    pieces = gather_terms(both, facets, chans)
    return finish(pieces, weights, transformed)


def solution(mesh):
    return jax.shard_map(
        local,
        mesh=mesh,
        in_specs=(
            P("facet", "chan", None, None),
            P(),
            P(),
            P(),
            P("facet"),
            P("facet", "chan", None, None),
        ),
        out_specs=P("facet", "chan", None),
        check_vma=False,
    )
```

```python
import functools
import math

import jax
import jax.numpy as jnp
from jax import lax
from jax.experimental import pallas as pl
from jax.experimental.pallas import tpu as pltpu
from jax.sharding import PartitionSpec as P

FACET = 8192
SIDE = 8
SKY = 65536
WIN = 64
TAYLOR = 4
LANE = 128
BLOCK = 256

SINE = (1.5707963705062866, -0.6459637880325317, 0.07968991994857788, -0.004674150608479977, 0.0001516751217423007)
COSINE = (0.9999999403953552, -1.2336982488632202, 0.2536506950855255, -0.020810570567846298, 0.0008581625297665596)


def turns(index):
    centred = ((index + SKY // 2) & (SKY - 1)) - SKY // 2
    z = centred.astype(jnp.float32) * (2.0 / SKY)
    w = z * z
    half_sin = z * (SINE[0] + w * (SINE[1] + w * (SINE[2] + w * (SINE[3] + w * SINE[4]))))
    half_cos = COSINE[0] + w * (COSINE[1] + w * (COSINE[2] + w * (COSINE[3] + w * COSINE[4])))
    return 1.0 - 2.0 * half_sin * half_sin, 2.0 * half_sin * half_cos


def grant(*arrays):
    return (8 << 20) + 2 * sum(4 * math.prod(array.shape) for array in arrays)


def lasting(microseconds):
    return pl.CostEstimate(flops=int(microseconds * 1.15e9), bytes_accessed=0, transcendentals=0)


def split(value):
    high = value.astype(jnp.bfloat16)
    return high, (value - high.astype(jnp.float32)).astype(jnp.bfloat16)


def rotate(real, imag, cosines, sines):
    return real * cosines + imag * sines, imag * cosines - real * sines


def write_tables(group, step, anchor, offset_ref, look_ref, turn_ref):
    count = group * WIN
    lane_index = lax.broadcasted_iota(jnp.int32, (1, count), 1)
    sublane = lax.broadcasted_iota(jnp.int32, (16, count), 0)
    hops = turn_ref.shape[0] // 2 - step
    shifts = [16, 32, 64] + [BLOCK * step << k for k in range(hops)] + [anchor + k * BLOCK for k in range(step)]
    shift = sum(jnp.where(sublane == k, value, 0) for k, value in enumerate(shifts))
    for first in range(0, offset_ref.shape[1], group):
        freq = lane_index % WIN
        for k in range(group):
            freq = freq + jnp.where(lane_index // WIN == k, offset_ref[0, first + k], 0)
        cosines, sines = turns(shift * freq)
        turned = [(cosines[k : k + 1], sines[k : k + 1]) for k in range(len(shifts))]
        cosines, sines = turns(sublane * freq)
        tables = [(cosines, -sines)]
        for k in range(2):
            tables = tables + [rotate(*table, *turned[k]) for table in tables]
        while len(tables) < BLOCK // 16:
            tables.append(rotate(*tables[-4], *turned[2]))
        for part in (0, 1):
            high, low = split(jnp.concatenate([table[part] for table in tables], axis=0))
            start = (2 * first + part * group) * WIN
            look_ref[0, :, start : start + count] = high
            look_ref[1, :, start : start + count] = low
        for k, hop in enumerate(turned[3:]):
            for part in (0, 1):
                turn_ref[2 * k + part : 2 * k + part + 1, first * WIN : first * WIN + count] = hop[part]


def columns(group, step, term_ref, look_ref, turn_ref):
    rows, width = term_ref.shape[2:]
    count = group * WIN
    tall = step * rows
    hops = turn_ref.shape[0] // 2 - step
    folded = jnp.concatenate([term_ref[0, 0, :, k * BLOCK : (k + 1) * BLOCK] for k in range(width // BLOCK)], axis=0)
    term_high, term_low = split(folded)
    dot = functools.partial(jnp.dot, preferred_element_type=jnp.float32)
    for first in range(0, turn_ref.shape[1] // WIN, group):
        start = 2 * first * WIN
        look_high = look_ref[0, :, start : start + 2 * count]
        look_low = look_ref[1, :, start : start + 2 * count]
        part = dot(term_high, look_high) + (dot(term_low, look_high) + dot(term_high, look_low))
        turn = [turn_ref[k : k + 1, first * WIN : first * WIN + count] for k in range(turn_ref.shape[0])]
        pieces = []
        for k in range(0, part.shape[0], tall):
            pieces.append((part[k : k + tall, :count], part[k : k + tall, count:]))
        for k in range(hops):
            merged = []
            for near, far in zip(pieces[::2], pieces[1::2]):
                moved = rotate(*far, turn[2 * k], turn[2 * k + 1])
                merged.append((near[0] + moved[0], near[1] + moved[1]))
            pieces = merged
        (real, imag), = pieces
        total_real = total_imag = 0.0
        for k in range(step):
            mine = slice(k * rows, (k + 1) * rows)
            piece = rotate(real[mine], imag[mine], turn[2 * (hops + k)], turn[2 * (hops + k) + 1])
            total_real, total_imag = total_real + piece[0], total_imag + piece[1]
        yield start, count, total_real, total_imag


def own_kernel(group, step, offset_hbm, term_hbm, look_ref, turn_ref, out_ref, *scratch):
    offset_ref, term_ref, sems = scratch
    moves = ((offset_hbm, offset_ref), (term_hbm, term_ref))
    copies = [pltpu.make_async_copy(a, b, sems.at[k]) for k, (a, b) in enumerate(moves)]
    for copy in copies:
        copy.start()
    anchor = lax.axis_index("facet") % SIDE * FACET
    copies[0].wait()
    write_tables(group, step, anchor, offset_ref, look_ref, turn_ref)
    copies[1].wait()
    for start, count, real, imag in columns(group, step, term_ref, look_ref, turn_ref):
        out_ref[:, start : start + count] = real
        out_ref[:, start + count : start + 2 * count] = imag


def other_kernel(group, step, term_ref, look_ref, turn_ref, own_ref, out_ref):
    rows = own_ref.shape[0]
    odd = lax.axis_index("chan") % 2 == 1
    for start, count, *other in columns(group, step, term_ref, look_ref, turn_ref):
        for k, value in enumerate(other):
            place = slice(start + k * count, start + (k + 1) * count)
            own = own_ref[:, place]
            out_ref[:rows, place] = jnp.where(odd, value, own)
            out_ref[rows:, place] = jnp.where(odd, own, value)


def own_columns(offsets, taylor):
    rows, width = taylor.shape[2:]
    subgrids = offsets.shape[1]
    step = max(8 // rows, 1)
    hops = (width // BLOCK // step).bit_length() - 1
    shapes = [
        jax.ShapeDtypeStruct((2, BLOCK, 2 * subgrids * WIN), jnp.bfloat16),
        jax.ShapeDtypeStruct((2 * (hops + step), subgrids * WIN), jnp.float32),
        jax.ShapeDtypeStruct((rows, 2 * subgrids * WIN), jnp.float32),
    ]
    return pl.pallas_call(
        functools.partial(own_kernel, math.gcd(subgrids, 4), step),
        in_specs=[pl.BlockSpec(memory_space=pltpu.HBM)] * 2,
        out_specs=[pl.BlockSpec(memory_space=pltpu.VMEM)] * 3,
        out_shape=shapes,
        scratch_shapes=[
            pltpu.SMEM(offsets.shape, jnp.int32),
            pltpu.VMEM(taylor.shape, jnp.float32),
            pltpu.SemaphoreType.DMA((2,)),
        ],
        cost_estimate=lasting(1.4),
        compiler_params=pltpu.CompilerParams(vmem_limit_bytes=grant(*shapes)),
        name="own_columns",
    )(*(pltpu.with_memory_space_constraint(array, pltpu.HBM) for array in (offsets, taylor)))


def both_columns(taylor, tables, own):
    rows = taylor.shape[2]
    columns_out = tables[0].shape[2]
    return pl.pallas_call(
        functools.partial(other_kernel, math.gcd(columns_out // (2 * WIN), 4), max(8 // rows, 1)),
        in_specs=[pl.BlockSpec(memory_space=pltpu.VMEM)] * 4,
        out_specs=pl.BlockSpec(memory_space=pltpu.VMEM),
        out_shape=jax.ShapeDtypeStruct((2 * rows, columns_out), jnp.float32),
        cost_estimate=lasting(0.35),
        compiler_params=pltpu.CompilerParams(vmem_limit_bytes=grant(taylor, *tables)),
        name="both_columns",
    )(taylor, *tables, own)


def exchange(value, facets, chans, flip_facet, flip_chan):
    pairs = [
        (f * chans + c, (f ^ flip_facet) * chans + (c ^ flip_chan)) for f in range(facets) for c in range(chans)
    ]
    return lax.ppermute(value, ("facet", "chan"), pairs)


def gather_channel(both, mix, facets, chans):
    near = SIDE if facets > SIDE else facets
    rows = both.shape[0] // 2
    step = 1
    while step < near:
        both = both + exchange(both, facets, chans, step, 1)
        step *= 2
    parts = []
    for k in range(chans // 2):
        weighted = both * mix[k]
        part = weighted[:rows] + weighted[rows:]
        parts.append(exchange(part, facets, chans, 0, 2 * k + 1) if k else part)
    if facets == near:
        return [part[None] for part in parts]
    groups = [[h * near + f for h in range(facets // near)] for f in range(near)]
    return [lax.all_gather(sum(parts), "facet", axis=0, axis_index_groups=groups)]


def weight_kernel(
    rows, offset_hbm, owner_hbm, tile_hbm, coord_hbm, fourier_hbm, row_ref, mask_ref, mix_ref, block_ref, *scratch
):
    hbm = (offset_hbm, owner_hbm, tile_hbm, coord_hbm, fourier_hbm)
    offset_ref, owner_ref, tile_ref, coord_ref, sems = scratch
    targets = (*scratch[:4], block_ref)
    copies = [pltpu.make_async_copy(a, b, sems.at[k]) for k, (a, b) in enumerate(zip(hbm, targets))]
    for copy in copies:
        copy.start()
    facets = lax.axis_size("facet")
    band, chan = lax.axis_index("facet"), lax.axis_index("chan")

    for copy in copies[:4]:
        copy.wait()

    blocks = tile_ref.shape[0]
    sublane = lax.broadcasted_iota(jnp.int32, (blocks, LANE), 0)
    lane = lax.broadcasted_iota(jnp.int32, (blocks, LANE), 1)
    tile = jnp.zeros((blocks, LANE), jnp.int32)
    for b in range(blocks):
        tile = jnp.where(sublane == b, tile_ref[b], tile)
    slot = jnp.where(tile < 0, -1, tile // WIN)
    first_row = jnp.zeros((blocks, LANE), jnp.int32)
    seen = jnp.int32(0)
    for pair in range(0, owner_ref.shape[0], LANE // WIN):
        mask = jnp.zeros((blocks, LANE), jnp.float32)
        for k in range(LANE // WIN):
            owned = owner_ref[pair + k] == band
            chosen = slot == jnp.where(owned, seen, -2)
            seen = seen + jnp.where(owned, 1, 0)
            first_row = jnp.where(chosen, offset_ref[1, pair + k], first_row)
            mask = jnp.where(chosen & (lane // WIN == k), 1.0, mask)
        mask_ref[:, pair * WIN : pair * WIN + LANE] = mask

    scale = float((FACET * rows * facets) ** -0.5)
    v = lane % WIN
    up = jnp.maximum(tile, 0) % WIN * v * (SKY // WIN)
    near = SIDE if facets > SIDE else facets
    for h in range(facets // near):
        for r in range(rows):
            position = h % SIDE * FACET + h // SIDE * rows + r
            cosines, sines = turns(up - (first_row + v) * position)
            for part, value in enumerate((cosines, sines)):
                total = jnp.sum(jnp.where(lane < WIN, value, 0.0), axis=1, keepdims=True) * scale
                row_ref[part, h * rows + r] = jnp.broadcast_to(total, (blocks, LANE))

    term = 2 * (chan // 2) + lax.broadcasted_iota(jnp.int32, (2 * rows, LANE), 0) // rows
    for k in range(mix_ref.shape[0]):
        coord = coord_ref[chan ^ (2 * k + 1) if k else chan]
        power = jnp.ones((2 * rows, LANE), jnp.float32)
        for degree in range(1, TAYLOR):
            power = jnp.where(term >= degree, power * coord, power)
        for start in range(0, mix_ref.shape[2], LANE):
            mix_ref[k, :, start : start + LANE] = power
    copies[4].wait()


def finish_weights(offsets, owner, tiles, coord, fourier, facets, chans, rows):
    subgrids = owner.shape[0]
    blocks = tiles.shape[0]
    near = SIDE if facets > SIDE else facets
    shapes = [
        jax.ShapeDtypeStruct((2, facets // near * rows, blocks, LANE), jnp.float32),
        jax.ShapeDtypeStruct((blocks, subgrids * WIN), jnp.float32),
        jax.ShapeDtypeStruct((chans // 2, 2 * rows, 2 * subgrids * WIN), jnp.float32),
        jax.ShapeDtypeStruct(fourier.shape, jnp.float32),
    ]
    return pl.pallas_call(
        functools.partial(weight_kernel, rows),
        in_specs=[pl.BlockSpec(memory_space=pltpu.HBM)] * 5,
        out_specs=[pl.BlockSpec(memory_space=pltpu.VMEM)] * 4,
        out_shape=shapes,
        scratch_shapes=[
            pltpu.SMEM(offsets.shape, jnp.int32),
            pltpu.SMEM(owner.shape, jnp.int32),
            pltpu.SMEM(tiles.shape, jnp.int32),
            pltpu.SMEM(coord.shape, jnp.float32),
            pltpu.SemaphoreType.DMA((5,)),
        ],
        cost_estimate=lasting(1.3),
        compiler_params=pltpu.CompilerParams(vmem_limit_bytes=grant(*shapes)),
        name="finish_weights",
    )(*(pltpu.with_memory_space_constraint(array, pltpu.HBM) for array in (offsets, owner, tiles, coord, fourier)))


def finish_kernel(pieces, *refs):
    piece_refs = refs[:pieces]
    row_ref, mask_ref, block_ref, out_ref = refs[pieces:]
    groups, rows, width = piece_refs[0].shape
    subgrids = mask_ref.shape[1] // WIN
    group = math.gcd(subgrids, 4)
    count = group * WIN
    blocks = mask_ref.shape[0]
    real_row = imag_row = 0.0
    for first in range(0, subgrids, group):
        start = 2 * first * WIN
        real_t = imag_t = 0.0
        for h in range(groups):
            mixed = sum(ref[h, :, start : start + 2 * count] for ref in piece_refs)
            for r in range(rows):
                real_a = jnp.tile(row_ref[0, h * rows + r], (1, count // LANE))
                imag_a = jnp.tile(row_ref[1, h * rows + r], (1, count // LANE))
                real_y, imag_y = mixed[r : r + 1, :count], mixed[r : r + 1, count:]
                real_t = real_t + (real_a * real_y - imag_a * imag_y)
                imag_t = imag_t + (real_a * imag_y + imag_a * real_y)
        mask = mask_ref[:, first * WIN : first * WIN + count]
        for k in range(0, count, LANE):
            real_row = real_row + (real_t * mask)[:, k : k + LANE]
            imag_row = imag_row + (imag_t * mask)[:, k : k + LANE]
    real_row, imag_row = (sum(pltpu.roll(value, k, 1) for k in range(0, LANE, WIN)) for value in (real_row, imag_row))
    lane = lax.broadcasted_iota(jnp.int32, (8, LANE), 1)
    keep = lane // WIN == lax.broadcasted_iota(jnp.int32, (8, LANE), 0) % 2
    here = lax.broadcasted_iota(jnp.int32, (8, block_ref.shape[2]), 0) // 2
    vis = block_ref.shape[2] // 2
    for first in range(0, blocks, 8):
        highs, lows = [], []
        for value in (real_row, imag_row):
            mine = jnp.where(keep, value[first : first + 8], 0.0)
            high = mine.astype(jnp.bfloat16).astype(jnp.float32)
            highs.append(jnp.concatenate([high, high], axis=1))
            lows.append(jnp.concatenate([mine - high, jnp.zeros_like(mine)], axis=1))
        left = jnp.concatenate(highs + lows, axis=0).astype(jnp.bfloat16)
        real_c, imag_c = 0.0, 0.0
        for b in range(4):
            wide = jnp.dot(left, block_ref[first // 2 + b], preferred_element_type=jnp.float32)
            real_c = jnp.where(here == b, wide[:8] + wide[16:24], real_c)
            imag_c = jnp.where(here == b, wide[8:16] + wide[24:], imag_c)
        real_v, imag_v = real_c[:, :vis] - imag_c[:, vis:], real_c[:, vis:] + imag_c[:, :vis]
        for b in range(8):
            out_ref[first + b, :, :vis] = real_v[b : b + 1]
            out_ref[first + b, :, vis:] = imag_v[b : b + 1]


def finish(pieces, weights, transformed):
    blocks, width = 2 * transformed.shape[0], transformed.shape[2]
    return pl.pallas_call(
        functools.partial(finish_kernel, len(pieces)),
        in_specs=[pl.BlockSpec(memory_space=pltpu.VMEM)] * (len(pieces) + 3),
        out_specs=pl.BlockSpec(memory_space=pltpu.VMEM),
        out_shape=jax.ShapeDtypeStruct((blocks, 1, width), jnp.float32),
        cost_estimate=lasting(1.3),
        compiler_params=pltpu.CompilerParams(vmem_limit_bytes=grant(*pieces, *weights, transformed)),
        name="finish",
    )(*pieces, *weights, transformed)


def block_kernel(fourier_ref, out_ref):
    vis = out_ref.shape[2] // 2
    here = lax.broadcasted_iota(jnp.int32, (2 * WIN, 2 * WIN), 0)
    there = lax.broadcasted_iota(jnp.int32, (2 * WIN, 2 * WIN), 1)
    cosines, sines = turns((here % WIN) * (there % WIN) * (SKY // WIN))
    sines = jnp.where(here < WIN, -sines, sines)
    table_high, table_low = split(jnp.where((here < WIN) == (there < WIN), cosines, sines) * (1.0 / WIN))
    dot = functools.partial(jnp.dot, preferred_element_type=jnp.float32)
    for b in range(0, fourier_ref.shape[0], 2):
        pair = [
            jnp.concatenate([fourier_ref[k, 0, :, :vis], fourier_ref[k, 0, :, vis:]], axis=0) for k in (b, b + 1)
        ]
        high, low = split(jnp.concatenate(pair, axis=1))
        done = dot(table_high, high) + (dot(table_low, high) + dot(table_high, low))
        for k in (0, 1):
            matrix = jnp.concatenate([done[:WIN, k * vis : (k + 1) * vis], done[WIN:, k * vis : (k + 1) * vis]], axis=1)
            high, low = split(matrix)
            out_ref[b // 2, WIN * k : WIN * (k + 1)] = high
            out_ref[b // 2, WIN * (k + 2) : WIN * (k + 3)] = low


def transform_blocks(fourier):
    blocks, _, _, width = fourier.shape
    vis = width // 2
    return pl.pallas_call(
        block_kernel,
        in_specs=[pl.BlockSpec(memory_space=pltpu.VMEM)],
        out_specs=pl.BlockSpec(memory_space=pltpu.VMEM),
        out_shape=jax.ShapeDtypeStruct((blocks // 2, 4 * WIN, 2 * vis), jnp.bfloat16),
        cost_estimate=lasting(0.7),
        compiler_params=pltpu.CompilerParams(vmem_limit_bytes=grant(fourier, fourier, fourier)),
        name="transform_blocks",
    )(fourier)


def local(taylor, chan_coord, sub_offset, sub_owner, tile_list, fourier):
    facets, chans = lax.axis_size("facet"), lax.axis_size("chan")
    offsets = sub_offset.T
    beside = exchange(taylor, facets, chans, 0, 1)
    *tables, own = own_columns(offsets, taylor)
    both = both_columns(beside, tables, own)
    row_weights, mask, mix, blocks = finish_weights(
        offsets, sub_owner, tile_list, chan_coord, fourier, facets, chans, taylor.shape[2]
    )
    transformed = transform_blocks(blocks)
    parts = gather_channel(both, mix, facets, chans)
    return finish(parts, (row_weights, mask), transformed)


def solution(mesh):
    return jax.shard_map(
        local,
        mesh=mesh,
        in_specs=(
            P("facet", "chan", None, None),
            P(),
            P(),
            P(),
            P("facet"),
            P("facet", "chan", None, None),
        ),
        out_specs=P("facet", "chan", None),
        check_vma=False,
    )
```

```python
import functools
import math

import jax
import jax.numpy as jnp
from jax import lax
from jax.experimental import pallas as pl
from jax.experimental.pallas import tpu as pltpu
from jax.sharding import PartitionSpec as P

FACET = 8192
SIDE = 8
SKY = 65536
WIN = 64
TAYLOR = 4
LANE = 128
BLOCK = 256

SINE = (1.5707963705062866, -0.6459637880325317, 0.07968991994857788, -0.004674150608479977, 0.0001516751217423007)
COSINE = (0.9999999403953552, -1.2336982488632202, 0.2536506950855255, -0.020810570567846298, 0.0008581625297665596)


def turns(index):
    centred = ((index + SKY // 2) & (SKY - 1)) - SKY // 2
    z = centred.astype(jnp.float32) * (2.0 / SKY)
    w = z * z
    half_sin = z * (SINE[0] + w * (SINE[1] + w * (SINE[2] + w * (SINE[3] + w * SINE[4]))))
    half_cos = COSINE[0] + w * (COSINE[1] + w * (COSINE[2] + w * (COSINE[3] + w * COSINE[4])))
    return 1.0 - 2.0 * half_sin * half_sin, 2.0 * half_sin * half_cos


def grant(*arrays):
    return (8 << 20) + 2 * sum(4 * math.prod(array.shape) for array in arrays)


def lasting(microseconds):
    return pl.CostEstimate(flops=int(microseconds * 1.15e9), bytes_accessed=0, transcendentals=0)


def split(value):
    high = value.astype(jnp.bfloat16)
    return high, (value - high.astype(jnp.float32)).astype(jnp.bfloat16)


def rotate(real, imag, cosines, sines):
    return real * cosines + imag * sines, imag * cosines - real * sines


def write_tables(group, step, anchor, offset_ref, look_ref, turn_ref):
    count = group * WIN
    lane_index = lax.broadcasted_iota(jnp.int32, (1, count), 1)
    sublane = lax.broadcasted_iota(jnp.int32, (16, count), 0)
    hops = turn_ref.shape[0] // 2 - step
    shifts = [16, 32, 64] + [BLOCK * step << k for k in range(hops)] + [anchor + k * BLOCK for k in range(step)]
    shift = sum(jnp.where(sublane == k, value, 0) for k, value in enumerate(shifts))
    for first in range(0, offset_ref.shape[1], group):
        freq = lane_index % WIN
        for k in range(group):
            freq = freq + jnp.where(lane_index // WIN == k, offset_ref[0, first + k], 0)
        cosines, sines = turns(shift * freq)
        turned = [(cosines[k : k + 1], sines[k : k + 1]) for k in range(len(shifts))]
        cosines, sines = turns(sublane * freq)
        tables = [(cosines, -sines)]
        for k in range(2):
            tables = tables + [rotate(*table, *turned[k]) for table in tables]
        while len(tables) < BLOCK // 16:
            tables.append(rotate(*tables[-4], *turned[2]))
        for part in (0, 1):
            high, low = split(jnp.concatenate([table[part] for table in tables], axis=0))
            start = (2 * first + part * group) * WIN
            look_ref[0, :, start : start + count] = high
            look_ref[1, :, start : start + count] = low
        for k, hop in enumerate(turned[3:]):
            for part in (0, 1):
                turn_ref[2 * k + part : 2 * k + part + 1, first * WIN : first * WIN + count] = hop[part]


def columns(group, step, term_ref, look_ref, turn_ref):
    rows, width = term_ref.shape[2:]
    count = group * WIN
    tall = step * rows
    hops = turn_ref.shape[0] // 2 - step
    folded = jnp.concatenate([term_ref[0, 0, :, k * BLOCK : (k + 1) * BLOCK] for k in range(width // BLOCK)], axis=0)
    term_high, term_low = split(folded)
    dot = functools.partial(jnp.dot, preferred_element_type=jnp.float32)
    for first in range(0, turn_ref.shape[1] // WIN, group):
        start = 2 * first * WIN
        look_high = look_ref[0, :, start : start + 2 * count]
        look_low = look_ref[1, :, start : start + 2 * count]
        part = dot(term_high, look_high) + (dot(term_low, look_high) + dot(term_high, look_low))
        turn = [turn_ref[k : k + 1, first * WIN : first * WIN + count] for k in range(turn_ref.shape[0])]
        pieces = []
        for k in range(0, part.shape[0], tall):
            pieces.append((part[k : k + tall, :count], part[k : k + tall, count:]))
        for k in range(hops):
            merged = []
            for near, far in zip(pieces[::2], pieces[1::2]):
                moved = rotate(*far, turn[2 * k], turn[2 * k + 1])
                merged.append((near[0] + moved[0], near[1] + moved[1]))
            pieces = merged
        (real, imag), = pieces
        total_real = total_imag = 0.0
        for k in range(step):
            mine = slice(k * rows, (k + 1) * rows)
            piece = rotate(real[mine], imag[mine], turn[2 * (hops + k)], turn[2 * (hops + k) + 1])
            total_real, total_imag = total_real + piece[0], total_imag + piece[1]
        yield start, count, total_real, total_imag


def own_kernel(group, step, offset_hbm, term_hbm, look_ref, turn_ref, out_ref, *scratch):
    offset_ref, term_ref, sems = scratch
    moves = ((offset_hbm, offset_ref), (term_hbm, term_ref))
    copies = [pltpu.make_async_copy(a, b, sems.at[k]) for k, (a, b) in enumerate(moves)]
    for copy in copies:
        copy.start()
    anchor = lax.axis_index("facet") % SIDE * FACET
    copies[0].wait()
    write_tables(group, step, anchor, offset_ref, look_ref, turn_ref)
    copies[1].wait()
    for start, count, real, imag in columns(group, step, term_ref, look_ref, turn_ref):
        out_ref[:, start : start + count] = real
        out_ref[:, start + count : start + 2 * count] = imag


def other_kernel(group, step, term_ref, look_ref, turn_ref, own_ref, out_ref):
    rows = own_ref.shape[0]
    odd = lax.axis_index("chan") % 2 == 1
    for start, count, *other in columns(group, step, term_ref, look_ref, turn_ref):
        for k, value in enumerate(other):
            place = slice(start + k * count, start + (k + 1) * count)
            own = own_ref[:, place]
            out_ref[:rows, place] = jnp.where(odd, value, own)
            out_ref[rows:, place] = jnp.where(odd, own, value)


def own_columns(offsets, taylor):
    rows, width = taylor.shape[2:]
    subgrids = offsets.shape[1]
    step = max(8 // rows, 1)
    hops = (width // BLOCK // step).bit_length() - 1
    shapes = [
        jax.ShapeDtypeStruct((2, BLOCK, 2 * subgrids * WIN), jnp.bfloat16),
        jax.ShapeDtypeStruct((2 * (hops + step), subgrids * WIN), jnp.float32),
        jax.ShapeDtypeStruct((rows, 2 * subgrids * WIN), jnp.float32),
    ]
    return pl.pallas_call(
        functools.partial(own_kernel, math.gcd(subgrids, 4), step),
        in_specs=[pl.BlockSpec(memory_space=pltpu.HBM)] * 2,
        out_specs=[pl.BlockSpec(memory_space=pltpu.VMEM)] * 3,
        out_shape=shapes,
        scratch_shapes=[
            pltpu.SMEM(offsets.shape, jnp.int32),
            pltpu.VMEM(taylor.shape, jnp.float32),
            pltpu.SemaphoreType.DMA((2,)),
        ],
        cost_estimate=lasting(1.4),
        compiler_params=pltpu.CompilerParams(vmem_limit_bytes=grant(*shapes)),
        name="own_columns",
    )(*(pltpu.with_memory_space_constraint(array, pltpu.HBM) for array in (offsets, taylor)))


def both_columns(taylor, tables, own):
    rows = taylor.shape[2]
    columns_out = tables[0].shape[2]
    return pl.pallas_call(
        functools.partial(other_kernel, math.gcd(columns_out // (2 * WIN), 4), max(8 // rows, 1)),
        in_specs=[pl.BlockSpec(memory_space=pltpu.VMEM)] * 4,
        out_specs=pl.BlockSpec(memory_space=pltpu.VMEM),
        out_shape=jax.ShapeDtypeStruct((2 * rows, columns_out), jnp.float32),
        cost_estimate=lasting(0.35),
        compiler_params=pltpu.CompilerParams(vmem_limit_bytes=grant(taylor, *tables)),
        name="both_columns",
    )(taylor, *tables, own)


def exchange(value, facets, chans, flip_facet, flip_chan):
    pairs = [
        (f * chans + c, (f ^ flip_facet) * chans + (c ^ flip_chan)) for f in range(facets) for c in range(chans)
    ]
    return lax.ppermute(value, ("facet", "chan"), pairs)


def gather_channel(both, mix, facets, chans):
    near = SIDE if facets > SIDE else facets
    rows = both.shape[0] // 2
    step = 1
    while step < near:
        both = both + exchange(both, facets, chans, step, 1)
        step *= 2
    parts = []
    for k in range(chans // 2):
        weighted = both * mix[k]
        part = weighted[:rows] + weighted[rows:]
        parts.append(exchange(part, facets, chans, 0, 2 * k + 1) if k else part)
    if facets == near:
        return [part[None] for part in parts]
    groups = [[h * near + f for h in range(facets // near)] for f in range(near)]
    return [lax.all_gather(sum(parts), "facet", axis=0, axis_index_groups=groups)]


def weight_kernel(
    rows, offset_hbm, owner_hbm, tile_hbm, coord_hbm, fourier_hbm, row_ref, mask_ref, mix_ref, block_ref, *scratch
):
    hbm = (offset_hbm, owner_hbm, tile_hbm, coord_hbm, fourier_hbm)
    offset_ref, owner_ref, tile_ref, coord_ref, sems = scratch
    targets = (*scratch[:4], block_ref)
    copies = [pltpu.make_async_copy(a, b, sems.at[k]) for k, (a, b) in enumerate(zip(hbm, targets))]
    for copy in copies:
        copy.start()
    facets = lax.axis_size("facet")
    band, chan = lax.axis_index("facet"), lax.axis_index("chan")

    for copy in copies[:4]:
        copy.wait()

    blocks = tile_ref.shape[0]
    sublane = lax.broadcasted_iota(jnp.int32, (blocks, LANE), 0)
    lane = lax.broadcasted_iota(jnp.int32, (blocks, LANE), 1)
    tile = jnp.zeros((blocks, LANE), jnp.int32)
    for b in range(blocks):
        tile = jnp.where(sublane == b, tile_ref[b], tile)
    slot = jnp.where(tile < 0, -1, tile // WIN)
    first_row = jnp.zeros((blocks, LANE), jnp.int32)
    seen = jnp.int32(0)
    for pair in range(0, owner_ref.shape[0], LANE // WIN):
        mask = jnp.zeros((blocks, LANE), jnp.float32)
        for k in range(LANE // WIN):
            owned = owner_ref[pair + k] == band
            chosen = slot == jnp.where(owned, seen, -2)
            seen = seen + jnp.where(owned, 1, 0)
            first_row = jnp.where(chosen, offset_ref[1, pair + k], first_row)
            mask = jnp.where(chosen & (lane // WIN == k), 1.0, mask)
        mask_ref[:, pair * WIN : pair * WIN + LANE] = mask

    scale = float((FACET * rows * facets) ** -0.5)
    v = lane % WIN
    up = jnp.maximum(tile, 0) % WIN * v * (SKY // WIN)
    near = SIDE if facets > SIDE else facets
    for h in range(facets // near):
        for r in range(rows):
            position = h % SIDE * FACET + h // SIDE * rows + r
            cosines, sines = turns(up - (first_row + v) * position)
            for part, value in enumerate((cosines, sines)):
                total = jnp.sum(jnp.where(lane < WIN, value, 0.0), axis=1, keepdims=True) * scale
                row_ref[part, h * rows + r] = jnp.broadcast_to(total, (blocks, LANE))

    term = 2 * (chan // 2) + lax.broadcasted_iota(jnp.int32, (2 * rows, LANE), 0) // rows
    for k in range(mix_ref.shape[0]):
        coord = coord_ref[chan ^ (2 * k + 1) if k else chan]
        power = jnp.ones((2 * rows, LANE), jnp.float32)
        for degree in range(1, TAYLOR):
            power = jnp.where(term >= degree, power * coord, power)
        for start in range(0, mix_ref.shape[2], LANE):
            mix_ref[k, :, start : start + LANE] = power
    copies[4].wait()


def finish_weights(offsets, owner, tiles, coord, fourier, facets, chans, rows):
    subgrids = owner.shape[0]
    blocks = tiles.shape[0]
    near = SIDE if facets > SIDE else facets
    shapes = [
        jax.ShapeDtypeStruct((2, facets // near * rows, blocks, LANE), jnp.float32),
        jax.ShapeDtypeStruct((blocks, subgrids * WIN), jnp.float32),
        jax.ShapeDtypeStruct((chans // 2, 2 * rows, 2 * subgrids * WIN), jnp.float32),
        jax.ShapeDtypeStruct(fourier.shape, jnp.float32),
    ]
    return pl.pallas_call(
        functools.partial(weight_kernel, rows),
        in_specs=[pl.BlockSpec(memory_space=pltpu.HBM)] * 5,
        out_specs=[pl.BlockSpec(memory_space=pltpu.VMEM)] * 4,
        out_shape=shapes,
        scratch_shapes=[
            pltpu.SMEM(offsets.shape, jnp.int32),
            pltpu.SMEM(owner.shape, jnp.int32),
            pltpu.SMEM(tiles.shape, jnp.int32),
            pltpu.SMEM(coord.shape, jnp.float32),
            pltpu.SemaphoreType.DMA((5,)),
        ],
        cost_estimate=lasting(1.3),
        compiler_params=pltpu.CompilerParams(vmem_limit_bytes=grant(*shapes)),
        name="finish_weights",
    )(*(pltpu.with_memory_space_constraint(array, pltpu.HBM) for array in (offsets, owner, tiles, coord, fourier)))


def finish_kernel(pieces, *refs):
    piece_refs = refs[:pieces]
    row_ref, mask_ref, block_ref, out_ref = refs[pieces:]
    groups, rows, width = piece_refs[0].shape
    subgrids = mask_ref.shape[1] // WIN
    group = math.gcd(subgrids, 4)
    count = group * WIN
    blocks = mask_ref.shape[0]
    real_row = imag_row = 0.0
    for first in range(0, subgrids, group):
        start = 2 * first * WIN
        real_t = imag_t = 0.0
        for h in range(groups):
            mixed = sum(ref[h, :, start : start + 2 * count] for ref in piece_refs)
            for r in range(rows):
                real_a = jnp.tile(row_ref[0, h * rows + r], (1, count // LANE))
                imag_a = jnp.tile(row_ref[1, h * rows + r], (1, count // LANE))
                real_y, imag_y = mixed[r : r + 1, :count], mixed[r : r + 1, count:]
                real_t = real_t + (real_a * real_y - imag_a * imag_y)
                imag_t = imag_t + (real_a * imag_y + imag_a * real_y)
        mask = mask_ref[:, first * WIN : first * WIN + count]
        for k in range(0, count, LANE):
            real_row = real_row + (real_t * mask)[:, k : k + LANE]
            imag_row = imag_row + (imag_t * mask)[:, k : k + LANE]
    real_row, imag_row = (sum(pltpu.roll(value, k, 1) for k in range(0, LANE, WIN)) for value in (real_row, imag_row))
    lane = lax.broadcasted_iota(jnp.int32, (8, LANE), 1)
    keep = lane // WIN == lax.broadcasted_iota(jnp.int32, (8, LANE), 0) % 2
    here = lax.broadcasted_iota(jnp.int32, (8, block_ref.shape[2]), 0) // 2
    vis = block_ref.shape[2] // 2
    lefts = []
    for first in range(0, blocks, 8):
        highs, lows = [], []
        for value in (real_row, imag_row):
            mine = jnp.where(keep, value[first : first + 8], 0.0)
            high = mine.astype(jnp.bfloat16).astype(jnp.float32)
            highs.append(jnp.concatenate([high, high], axis=1))
            lows.append(jnp.concatenate([mine - high, jnp.zeros_like(mine)], axis=1))
        lefts.append(jnp.concatenate(highs + lows, axis=0).astype(jnp.bfloat16))
    reals, imags = [0.0] * len(lefts), [0.0] * len(lefts)
    for b in range(4):
        for k, left in enumerate(lefts):
            wide = jnp.dot(left, block_ref[4 * k + b], preferred_element_type=jnp.float32)
            reals[k] = jnp.where(here == b, wide[:8] + wide[16:24], reals[k])
            imags[k] = jnp.where(here == b, wide[8:16] + wide[24:], imags[k])
    for k, (real_c, imag_c) in enumerate(zip(reals, imags)):
        real_v, imag_v = real_c[:, :vis] - imag_c[:, vis:], real_c[:, vis:] + imag_c[:, :vis]
        for b in range(8):
            out_ref[8 * k + b, :, :vis] = real_v[b : b + 1]
            out_ref[8 * k + b, :, vis:] = imag_v[b : b + 1]


def finish(pieces, weights, transformed):
    blocks, width = 2 * transformed.shape[0], transformed.shape[2]
    return pl.pallas_call(
        functools.partial(finish_kernel, len(pieces)),
        in_specs=[pl.BlockSpec(memory_space=pltpu.VMEM)] * (len(pieces) + 3),
        out_specs=pl.BlockSpec(memory_space=pltpu.VMEM),
        out_shape=jax.ShapeDtypeStruct((blocks, 1, width), jnp.float32),
        cost_estimate=lasting(1.3),
        compiler_params=pltpu.CompilerParams(vmem_limit_bytes=grant(*pieces, *weights, transformed)),
        name="finish",
    )(*pieces, *weights, transformed)


def block_kernel(fourier_ref, out_ref):
    vis = out_ref.shape[2] // 2
    here = lax.broadcasted_iota(jnp.int32, (2 * WIN, 2 * WIN), 0)
    there = lax.broadcasted_iota(jnp.int32, (2 * WIN, 2 * WIN), 1)
    cosines, sines = turns((here % WIN) * (there % WIN) * (SKY // WIN))
    sines = jnp.where(here < WIN, -sines, sines)
    table_high, table_low = split(jnp.where((here < WIN) == (there < WIN), cosines, sines) * (1.0 / WIN))
    dot = functools.partial(jnp.dot, preferred_element_type=jnp.float32)
    for b in range(0, fourier_ref.shape[0], 2):
        pair = [
            jnp.concatenate([fourier_ref[k, 0, :, :vis], fourier_ref[k, 0, :, vis:]], axis=0) for k in (b, b + 1)
        ]
        high, low = split(jnp.concatenate(pair, axis=1))
        done = dot(table_high, high) + (dot(table_low, high) + dot(table_high, low))
        for k in (0, 1):
            matrix = jnp.concatenate([done[:WIN, k * vis : (k + 1) * vis], done[WIN:, k * vis : (k + 1) * vis]], axis=1)
            high, low = split(matrix)
            out_ref[b // 2, WIN * k : WIN * (k + 1)] = high
            out_ref[b // 2, WIN * (k + 2) : WIN * (k + 3)] = low


def transform_blocks(fourier):
    blocks, _, _, width = fourier.shape
    vis = width // 2
    return pl.pallas_call(
        block_kernel,
        in_specs=[pl.BlockSpec(memory_space=pltpu.VMEM)],
        out_specs=pl.BlockSpec(memory_space=pltpu.VMEM),
        out_shape=jax.ShapeDtypeStruct((blocks // 2, 4 * WIN, 2 * vis), jnp.bfloat16),
        cost_estimate=lasting(0.7),
        compiler_params=pltpu.CompilerParams(vmem_limit_bytes=grant(fourier, fourier, fourier)),
        name="transform_blocks",
    )(fourier)


def local(taylor, chan_coord, sub_offset, sub_owner, tile_list, fourier):
    facets, chans = lax.axis_size("facet"), lax.axis_size("chan")
    offsets = sub_offset.T
    beside = exchange(taylor, facets, chans, 0, 1)
    *tables, own = own_columns(offsets, taylor)
    both = both_columns(beside, tables, own)
    row_weights, mask, mix, blocks = finish_weights(
        offsets, sub_owner, tile_list, chan_coord, fourier, facets, chans, taylor.shape[2]
    )
    transformed = transform_blocks(blocks)
    parts = gather_channel(both, mix, facets, chans)
    return finish(parts, (row_weights, mask), transformed)


def solution(mesh):
    return jax.shard_map(
        local,
        mesh=mesh,
        in_specs=(
            P("facet", "chan", None, None),
            P(),
            P(),
            P(),
            P("facet"),
            P("facet", "chan", None, None),
        ),
        out_specs=P("facet", "chan", None),
        check_vma=False,
    )
```

```python
import functools
import math

import jax
import jax.numpy as jnp
from jax import lax
from jax.experimental import pallas as pl
from jax.experimental.pallas import tpu as pltpu
from jax.sharding import PartitionSpec as P

FACET = 8192
SIDE = 8
SKY = 65536
WIN = 64
TAYLOR = 4
LANE = 128
BLOCK = 256

SINE = (1.5707963705062866, -0.6459637880325317, 0.07968991994857788, -0.004674150608479977, 0.0001516751217423007)
COSINE = (0.9999999403953552, -1.2336982488632202, 0.2536506950855255, -0.020810570567846298, 0.0008581625297665596)


def turns(index):
    centred = ((index + SKY // 2) & (SKY - 1)) - SKY // 2
    z = centred.astype(jnp.float32) * (2.0 / SKY)
    w = z * z
    half_sin = z * (SINE[0] + w * (SINE[1] + w * (SINE[2] + w * (SINE[3] + w * SINE[4]))))
    half_cos = COSINE[0] + w * (COSINE[1] + w * (COSINE[2] + w * (COSINE[3] + w * COSINE[4])))
    return 1.0 - 2.0 * half_sin * half_sin, 2.0 * half_sin * half_cos


def grant(*arrays):
    return (8 << 20) + 2 * sum(4 * math.prod(array.shape) for array in arrays)


def lasting(microseconds):
    return pl.CostEstimate(flops=int(microseconds * 1.15e9), bytes_accessed=0, transcendentals=0)


def split(value):
    high = value.astype(jnp.bfloat16)
    return high, (value - high.astype(jnp.float32)).astype(jnp.bfloat16)


def rotate(real, imag, cosines, sines):
    return real * cosines + imag * sines, imag * cosines - real * sines


def write_tables(group, step, anchor, offset_ref, look_ref, turn_ref):
    count = group * WIN
    lane_index = lax.broadcasted_iota(jnp.int32, (1, count), 1)
    sublane = lax.broadcasted_iota(jnp.int32, (16, count), 0)
    hops = turn_ref.shape[0] // 2 - step
    shifts = [16, 32, 64] + [BLOCK * step << k for k in range(hops)] + [anchor + k * BLOCK for k in range(step)]
    shift = sum(jnp.where(sublane == k, value, 0) for k, value in enumerate(shifts))
    for first in range(0, offset_ref.shape[1], group):
        freq = lane_index % WIN
        for k in range(group):
            freq = freq + jnp.where(lane_index // WIN == k, offset_ref[0, first + k], 0)
        cosines, sines = turns(shift * freq)
        turned = [(cosines[k : k + 1], sines[k : k + 1]) for k in range(len(shifts))]
        cosines, sines = turns(sublane * freq)
        tables = [(cosines, -sines)]
        for k in range(2):
            tables = tables + [rotate(*table, *turned[k]) for table in tables]
        while len(tables) < BLOCK // 16:
            tables.append(rotate(*tables[-4], *turned[2]))
        for part in (0, 1):
            high, low = split(jnp.concatenate([table[part] for table in tables], axis=0))
            start = (2 * first + part * group) * WIN
            look_ref[0, :, start : start + count] = high
            look_ref[1, :, start : start + count] = low
        for k, hop in enumerate(turned[3:]):
            for part in (0, 1):
                turn_ref[2 * k + part : 2 * k + part + 1, first * WIN : first * WIN + count] = hop[part]


def columns(group, step, term_ref, look_ref, turn_ref):
    rows, width = term_ref.shape[2:]
    count = group * WIN
    tall = step * rows
    hops = turn_ref.shape[0] // 2 - step
    folded = jnp.concatenate([term_ref[0, 0, :, k * BLOCK : (k + 1) * BLOCK] for k in range(width // BLOCK)], axis=0)
    term_high, term_low = split(folded)
    dot = functools.partial(jnp.dot, preferred_element_type=jnp.float32)
    for first in range(0, turn_ref.shape[1] // WIN, group):
        start = 2 * first * WIN
        look_high = look_ref[0, :, start : start + 2 * count]
        look_low = look_ref[1, :, start : start + 2 * count]
        part = dot(term_high, look_high) + (dot(term_low, look_high) + dot(term_high, look_low))
        turn = [turn_ref[k : k + 1, first * WIN : first * WIN + count] for k in range(turn_ref.shape[0])]
        pieces = []
        for k in range(0, part.shape[0], tall):
            pieces.append((part[k : k + tall, :count], part[k : k + tall, count:]))
        for k in range(hops):
            merged = []
            for near, far in zip(pieces[::2], pieces[1::2]):
                moved = rotate(*far, turn[2 * k], turn[2 * k + 1])
                merged.append((near[0] + moved[0], near[1] + moved[1]))
            pieces = merged
        (real, imag), = pieces
        total_real = total_imag = 0.0
        for k in range(step):
            mine = slice(k * rows, (k + 1) * rows)
            piece = rotate(real[mine], imag[mine], turn[2 * (hops + k)], turn[2 * (hops + k) + 1])
            total_real, total_imag = total_real + piece[0], total_imag + piece[1]
        yield start, count, total_real, total_imag


def own_kernel(group, step, offset_hbm, term_hbm, look_ref, turn_ref, out_ref, *scratch):
    offset_ref, term_ref, sems = scratch
    moves = ((offset_hbm, offset_ref), (term_hbm, term_ref))
    copies = [pltpu.make_async_copy(a, b, sems.at[k]) for k, (a, b) in enumerate(moves)]
    for copy in copies:
        copy.start()
    anchor = lax.axis_index("facet") % SIDE * FACET
    copies[0].wait()
    write_tables(group, step, anchor, offset_ref, look_ref, turn_ref)
    copies[1].wait()
    for start, count, real, imag in columns(group, step, term_ref, look_ref, turn_ref):
        out_ref[:, start : start + count] = real
        out_ref[:, start + count : start + 2 * count] = imag


def other_kernel(group, step, term_ref, look_ref, turn_ref, own_ref, out_ref):
    rows = own_ref.shape[0]
    odd = lax.axis_index("chan") % 2 == 1
    for start, count, *other in columns(group, step, term_ref, look_ref, turn_ref):
        for k, value in enumerate(other):
            place = slice(start + k * count, start + (k + 1) * count)
            own = own_ref[:, place]
            out_ref[:rows, place] = jnp.where(odd, value, own)
            out_ref[rows:, place] = jnp.where(odd, own, value)


def own_columns(offsets, taylor):
    rows, width = taylor.shape[2:]
    subgrids = offsets.shape[1]
    step = max(8 // rows, 1)
    hops = (width // BLOCK // step).bit_length() - 1
    shapes = [
        jax.ShapeDtypeStruct((2, BLOCK, 2 * subgrids * WIN), jnp.bfloat16),
        jax.ShapeDtypeStruct((2 * (hops + step), subgrids * WIN), jnp.float32),
        jax.ShapeDtypeStruct((rows, 2 * subgrids * WIN), jnp.float32),
    ]
    return pl.pallas_call(
        functools.partial(own_kernel, math.gcd(subgrids, 4), step),
        in_specs=[pl.BlockSpec(memory_space=pltpu.HBM)] * 2,
        out_specs=[pl.BlockSpec(memory_space=pltpu.VMEM)] * 3,
        out_shape=shapes,
        scratch_shapes=[
            pltpu.SMEM(offsets.shape, jnp.int32),
            pltpu.VMEM(taylor.shape, jnp.float32),
            pltpu.SemaphoreType.DMA((2,)),
        ],
        cost_estimate=lasting(1.4),
        compiler_params=pltpu.CompilerParams(vmem_limit_bytes=grant(*shapes)),
        name="own_columns",
    )(*(pltpu.with_memory_space_constraint(array, pltpu.HBM) for array in (offsets, taylor)))


def both_columns(taylor, tables, own):
    rows = taylor.shape[2]
    columns_out = tables[0].shape[2]
    return pl.pallas_call(
        functools.partial(other_kernel, math.gcd(columns_out // (2 * WIN), 4), max(8 // rows, 1)),
        in_specs=[pl.BlockSpec(memory_space=pltpu.VMEM)] * 4,
        out_specs=pl.BlockSpec(memory_space=pltpu.VMEM),
        out_shape=jax.ShapeDtypeStruct((2 * rows, columns_out), jnp.float32),
        cost_estimate=lasting(0.35),
        compiler_params=pltpu.CompilerParams(vmem_limit_bytes=grant(taylor, *tables)),
        name="both_columns",
    )(taylor, *tables, own)


def exchange(value, facets, chans, flip_facet, flip_chan):
    pairs = [
        (f * chans + c, (f ^ flip_facet) * chans + (c ^ flip_chan)) for f in range(facets) for c in range(chans)
    ]
    return lax.ppermute(value, ("facet", "chan"), pairs)


def gather_channel(both, mix, facets, chans):
    near = SIDE if facets > SIDE else facets
    rows = both.shape[0] // 2
    step = near
    while step > 1:
        step //= 2
        both = both + exchange(both, facets, chans, step, 1)
    parts = []
    for k in range(chans // 2):
        weighted = both * mix[k]
        part = weighted[:rows] + weighted[rows:]
        parts.append(exchange(part, facets, chans, 0, 2 * k + 1) if k else part)
    if facets == near:
        return [part[None] for part in parts]
    groups = [[h * near + f for h in range(facets // near)] for f in range(near)]
    return [lax.all_gather(sum(parts), "facet", axis=0, axis_index_groups=groups)]


def weight_kernel(
    rows, offset_hbm, owner_hbm, tile_hbm, coord_hbm, fourier_hbm, row_ref, mask_ref, mix_ref, block_ref, *scratch
):
    hbm = (offset_hbm, owner_hbm, tile_hbm, coord_hbm, fourier_hbm)
    offset_ref, owner_ref, tile_ref, coord_ref, sems = scratch
    targets = (*scratch[:4], block_ref)
    copies = [pltpu.make_async_copy(a, b, sems.at[k]) for k, (a, b) in enumerate(zip(hbm, targets))]
    for copy in copies:
        copy.start()
    facets = lax.axis_size("facet")
    band, chan = lax.axis_index("facet"), lax.axis_index("chan")

    for copy in copies[:4]:
        copy.wait()

    blocks = tile_ref.shape[0]
    sublane = lax.broadcasted_iota(jnp.int32, (blocks, LANE), 0)
    lane = lax.broadcasted_iota(jnp.int32, (blocks, LANE), 1)
    tile = jnp.zeros((blocks, LANE), jnp.int32)
    for b in range(blocks):
        tile = jnp.where(sublane == b, tile_ref[b], tile)
    slot = jnp.where(tile < 0, -1, tile // WIN)
    first_row = jnp.zeros((blocks, LANE), jnp.int32)
    seen = jnp.int32(0)
    for pair in range(0, owner_ref.shape[0], LANE // WIN):
        mask = jnp.zeros((blocks, LANE), jnp.float32)
        for k in range(LANE // WIN):
            owned = owner_ref[pair + k] == band
            chosen = slot == jnp.where(owned, seen, -2)
            seen = seen + jnp.where(owned, 1, 0)
            first_row = jnp.where(chosen, offset_ref[1, pair + k], first_row)
            mask = jnp.where(chosen & (lane // WIN == k), 1.0, mask)
        mask_ref[:, pair * WIN : pair * WIN + LANE] = mask

    scale = float((FACET * rows * facets) ** -0.5)
    v = lane % WIN
    up = jnp.maximum(tile, 0) % WIN * v * (SKY // WIN)
    near = SIDE if facets > SIDE else facets
    for h in range(facets // near):
        for r in range(rows):
            position = h % SIDE * FACET + h // SIDE * rows + r
            cosines, sines = turns(up - (first_row + v) * position)
            for part, value in enumerate((cosines, sines)):
                total = jnp.sum(jnp.where(lane < WIN, value, 0.0), axis=1, keepdims=True) * scale
                row_ref[part, h * rows + r] = jnp.broadcast_to(total, (blocks, LANE))

    term = 2 * (chan // 2) + lax.broadcasted_iota(jnp.int32, (2 * rows, LANE), 0) // rows
    for k in range(mix_ref.shape[0]):
        coord = coord_ref[chan ^ (2 * k + 1) if k else chan]
        power = jnp.ones((2 * rows, LANE), jnp.float32)
        for degree in range(1, TAYLOR):
            power = jnp.where(term >= degree, power * coord, power)
        for start in range(0, mix_ref.shape[2], LANE):
            mix_ref[k, :, start : start + LANE] = power
    copies[4].wait()


def finish_weights(offsets, owner, tiles, coord, fourier, facets, chans, rows):
    subgrids = owner.shape[0]
    blocks = tiles.shape[0]
    near = SIDE if facets > SIDE else facets
    shapes = [
        jax.ShapeDtypeStruct((2, facets // near * rows, blocks, LANE), jnp.float32),
        jax.ShapeDtypeStruct((blocks, subgrids * WIN), jnp.float32),
        jax.ShapeDtypeStruct((chans // 2, 2 * rows, 2 * subgrids * WIN), jnp.float32),
        jax.ShapeDtypeStruct(fourier.shape, jnp.float32),
    ]
    return pl.pallas_call(
        functools.partial(weight_kernel, rows),
        in_specs=[pl.BlockSpec(memory_space=pltpu.HBM)] * 5,
        out_specs=[pl.BlockSpec(memory_space=pltpu.VMEM)] * 4,
        out_shape=shapes,
        scratch_shapes=[
            pltpu.SMEM(offsets.shape, jnp.int32),
            pltpu.SMEM(owner.shape, jnp.int32),
            pltpu.SMEM(tiles.shape, jnp.int32),
            pltpu.SMEM(coord.shape, jnp.float32),
            pltpu.SemaphoreType.DMA((5,)),
        ],
        cost_estimate=lasting(1.3),
        compiler_params=pltpu.CompilerParams(vmem_limit_bytes=grant(*shapes)),
        name="finish_weights",
    )(*(pltpu.with_memory_space_constraint(array, pltpu.HBM) for array in (offsets, owner, tiles, coord, fourier)))


def finish_kernel(pieces, *refs):
    piece_refs = refs[:pieces]
    row_ref, mask_ref, block_ref, out_ref = refs[pieces:]
    groups, rows, width = piece_refs[0].shape
    subgrids = mask_ref.shape[1] // WIN
    group = math.gcd(subgrids, 4)
    count = group * WIN
    blocks = mask_ref.shape[0]
    real_row = imag_row = 0.0
    for first in range(0, subgrids, group):
        start = 2 * first * WIN
        real_t = imag_t = 0.0
        for h in range(groups):
            mixed = sum(ref[h, :, start : start + 2 * count] for ref in piece_refs)
            for r in range(rows):
                real_a = jnp.tile(row_ref[0, h * rows + r], (1, count // LANE))
                imag_a = jnp.tile(row_ref[1, h * rows + r], (1, count // LANE))
                real_y, imag_y = mixed[r : r + 1, :count], mixed[r : r + 1, count:]
                real_t = real_t + (real_a * real_y - imag_a * imag_y)
                imag_t = imag_t + (real_a * imag_y + imag_a * real_y)
        mask = mask_ref[:, first * WIN : first * WIN + count]
        for k in range(0, count, LANE):
            real_row = real_row + (real_t * mask)[:, k : k + LANE]
            imag_row = imag_row + (imag_t * mask)[:, k : k + LANE]
    real_row, imag_row = (sum(pltpu.roll(value, k, 1) for k in range(0, LANE, WIN)) for value in (real_row, imag_row))
    lane = lax.broadcasted_iota(jnp.int32, (8, LANE), 1)
    keep = lane // WIN == lax.broadcasted_iota(jnp.int32, (8, LANE), 0) % 2
    here = lax.broadcasted_iota(jnp.int32, (8, block_ref.shape[2]), 0) // 2
    vis = block_ref.shape[2] // 2
    lefts = []
    for first in range(0, blocks, 8):
        highs, lows = [], []
        for value in (real_row, imag_row):
            mine = jnp.where(keep, value[first : first + 8], 0.0)
            high = mine.astype(jnp.bfloat16).astype(jnp.float32)
            highs.append(jnp.concatenate([high, high], axis=1))
            lows.append(jnp.concatenate([mine - high, jnp.zeros_like(mine)], axis=1))
        lefts.append(jnp.concatenate(highs + lows, axis=0).astype(jnp.bfloat16))
    reals, imags = [0.0] * len(lefts), [0.0] * len(lefts)
    for b in range(4):
        for k, left in enumerate(lefts):
            wide = jnp.dot(left, block_ref[4 * k + b], preferred_element_type=jnp.float32)
            reals[k] = jnp.where(here == b, wide[:8] + wide[16:24], reals[k])
            imags[k] = jnp.where(here == b, wide[8:16] + wide[24:], imags[k])
    for k, (real_c, imag_c) in enumerate(zip(reals, imags)):
        real_v, imag_v = real_c[:, :vis] - imag_c[:, vis:], real_c[:, vis:] + imag_c[:, :vis]
        for b in range(8):
            out_ref[8 * k + b, :, :vis] = real_v[b : b + 1]
            out_ref[8 * k + b, :, vis:] = imag_v[b : b + 1]


def finish(pieces, weights, transformed):
    blocks, width = 2 * transformed.shape[0], transformed.shape[2]
    return pl.pallas_call(
        functools.partial(finish_kernel, len(pieces)),
        in_specs=[pl.BlockSpec(memory_space=pltpu.VMEM)] * (len(pieces) + 3),
        out_specs=pl.BlockSpec(memory_space=pltpu.VMEM),
        out_shape=jax.ShapeDtypeStruct((blocks, 1, width), jnp.float32),
        cost_estimate=lasting(1.3),
        compiler_params=pltpu.CompilerParams(vmem_limit_bytes=grant(*pieces, *weights, transformed)),
        name="finish",
    )(*pieces, *weights, transformed)


def block_kernel(fourier_ref, out_ref):
    vis = out_ref.shape[2] // 2
    here = lax.broadcasted_iota(jnp.int32, (2 * WIN, 2 * WIN), 0)
    there = lax.broadcasted_iota(jnp.int32, (2 * WIN, 2 * WIN), 1)
    cosines, sines = turns((here % WIN) * (there % WIN) * (SKY // WIN))
    sines = jnp.where(here < WIN, -sines, sines)
    table_high, table_low = split(jnp.where((here < WIN) == (there < WIN), cosines, sines) * (1.0 / WIN))
    dot = functools.partial(jnp.dot, preferred_element_type=jnp.float32)
    for b in range(0, fourier_ref.shape[0], 2):
        pair = [
            jnp.concatenate([fourier_ref[k, 0, :, :vis], fourier_ref[k, 0, :, vis:]], axis=0) for k in (b, b + 1)
        ]
        high, low = split(jnp.concatenate(pair, axis=1))
        done = dot(table_high, high) + (dot(table_low, high) + dot(table_high, low))
        for k in (0, 1):
            matrix = jnp.concatenate([done[:WIN, k * vis : (k + 1) * vis], done[WIN:, k * vis : (k + 1) * vis]], axis=1)
            high, low = split(matrix)
            out_ref[b // 2, WIN * k : WIN * (k + 1)] = high
            out_ref[b // 2, WIN * (k + 2) : WIN * (k + 3)] = low


def transform_blocks(fourier):
    blocks, _, _, width = fourier.shape
    vis = width // 2
    return pl.pallas_call(
        block_kernel,
        in_specs=[pl.BlockSpec(memory_space=pltpu.VMEM)],
        out_specs=pl.BlockSpec(memory_space=pltpu.VMEM),
        out_shape=jax.ShapeDtypeStruct((blocks // 2, 4 * WIN, 2 * vis), jnp.bfloat16),
        cost_estimate=lasting(0.7),
        compiler_params=pltpu.CompilerParams(vmem_limit_bytes=grant(fourier, fourier, fourier)),
        name="transform_blocks",
    )(fourier)


def local(taylor, chan_coord, sub_offset, sub_owner, tile_list, fourier):
    facets, chans = lax.axis_size("facet"), lax.axis_size("chan")
    offsets = sub_offset.T
    beside = exchange(taylor, facets, chans, 0, 1)
    *tables, own = own_columns(offsets, taylor)
    both = both_columns(beside, tables, own)
    row_weights, mask, mix, blocks = finish_weights(
        offsets, sub_owner, tile_list, chan_coord, fourier, facets, chans, taylor.shape[2]
    )
    transformed = transform_blocks(blocks)
    parts = gather_channel(both, mix, facets, chans)
    return finish(parts, (row_weights, mask), transformed)


def solution(mesh):
    return jax.shard_map(
        local,
        mesh=mesh,
        in_specs=(
            P("facet", "chan", None, None),
            P(),
            P(),
            P(),
            P("facet"),
            P("facet", "chan", None, None),
        ),
        out_specs=P("facet", "chan", None),
        check_vma=False,
    )
```
